256 devices in a mesh: layer: 16 (over x, y), slab: 16 (over z, core).
Axes of the slice: x: 4, y: 4, z: 8, core: 2. Of those that a mesh axis runs over, the one named last changes fastest.
Arguments:
- labels: int32 [32768, 2048], P(('layer', 'slab')), parts along dimension 0, may hold values from 0 to 3
Outputs:
- q_panel: float32 [2, 16384, 20402], P(None, ('layer', 'slab')), parts along dimension 1
The draws below stay inside these ranges and needn't reach their ends.
There are 16 independent parts, one for each index of `layer`. The reference program is written for one: setup_inputs(seed, part) draws one part's arguments, and reference() takes and returns one part's arrays. A program takes and returns all parts, laid end to end along the dimension named above; each array names one. Nothing has to cross between parts.
All inputs are finite; a program needn't handle non-finite values.
Results may differ from the reference program's by a relative error of at most 0.0003.
Values sent between devices are 32-bit elements; how exact they have to be, the bound alone decides.
A program may use at most 192 MiB of HBM per device.

```python
import jax
import jax.numpy as jnp
from jax import lax

NMAP = 2048
HARM = 101
ROWS_DEV = 64
KEEP = 201
ORDERS = 10201
N_SLAB = 16


def draw_labels(key, part):
    key_rows, key_cols, key_table = jax.random.split(key, 3)
    cut_count = max(NMAP // 24, 4)
    row_cuts = jax.random.randint(key_rows, (cut_count,), 0, NMAP)
    col_cuts = jax.random.randint(key_cols, (cut_count,), 0, NMAP)
    places = jnp.arange(NMAP, dtype=jnp.int32)
    row_block = jnp.sum((places[:, None] >= row_cuts[None, :]).astype(jnp.int32), axis=1)
    col_block = jnp.sum((places[:, None] >= col_cuts[None, :]).astype(jnp.int32), axis=1)
    table = jax.random.randint(key_table, (cut_count + 1, cut_count + 1), 0, 4)
    labels = table[row_block[:, None], col_block[None, :]]
    labels = labels.at[0, 0].set(3).at[0, 1].set(0)
    return labels.astype(jnp.int32)


def setup_inputs(seed: int = 0, part: int = 0) -> dict:
    keys = jax.random.split(jax.random.key(seed), 2)
    part_keys = jax.random.split(jax.random.fold_in(keys[1], part), 2)
    return {
        "labels": draw_labels(jax.random.fold_in(jax.random.fold_in(keys[1], part), 71), part),
    }


PERMITS = (1.0, 2.1, 4.0, 12.1)

def permittivity(labels):
    total = jnp.zeros(labels.shape, jnp.float32)
    for index_value in range(4):
        total = total + jnp.where(labels == index_value, jnp.float32(PERMITS[index_value]), jnp.float32(0.0))
    return total

def smooth_all(field_in):
    return (4.0 * field_in + jnp.roll(field_in, 1, 0) + jnp.roll(field_in, -1, 0) + jnp.roll(field_in, 1, 1) + jnp.roll(field_in, -1, 1)) / 8.0

def field_stack(labels):
    permit = permittivity(labels)
    smooth = permit
    for sweep_index in range(3):
        smooth = smooth_all(smooth)
    grad_x = (jnp.roll(smooth, -1, 0) - jnp.roll(smooth, 1, 0)) / 2.0
    grad_y = (jnp.roll(smooth, -1, 1) - jnp.roll(smooth, 1, 1)) / 2.0
    scale = jnp.sqrt(grad_x * grad_x + grad_y * grad_y + 1.0)
    normal_x = grad_x / scale
    normal_y = grad_y / scale
    inverse = 1.0 / permit
    contrast = permit - inverse
    return jnp.stack([permit, contrast * normal_x * normal_x, contrast * normal_x * normal_y, contrast * normal_y * normal_y])

def build_rows(coefficients, window_rows, spacing):
    flipped = coefficients[:, :, ::-1, ::-1]
    centre = (HARM - 1) // 2
    order_count = HARM * HARM

    def one_row(row_index):
        lower_half = row_index % 2
        order_index = row_index // 2 * spacing
        first_index = order_index // HARM
        second = order_index % HARM
        zero_start = jnp.zeros((), jnp.int32)
        window = lax.dynamic_slice(flipped, (zero_start, zero_start, (HARM - 1 - first_index).astype(jnp.int32), (HARM - 1 - second).astype(jnp.int32)), (2, 4, HARM, HARM))
        toeplitz = window.reshape(2, 4, order_count)
        kx_row = 0.3 + 0.02 * (first_index - centre).astype(jnp.float32)
        ky_row = 0.2 + 0.02 * (second - centre).astype(jnp.float32)
        diag_real = (jnp.arange(order_count, dtype=jnp.int32) == order_index).astype(jnp.float32)
        diag_pair = jnp.stack([diag_real, jnp.zeros_like(diag_real)])
        top_left = kx_row * ky_row * diag_pair + toeplitz[:, 2]
        top_right = toeplitz[:, 0] - toeplitz[:, 3] - kx_row * kx_row * diag_pair
        low_left = ky_row * ky_row * diag_pair - toeplitz[:, 0] + toeplitz[:, 1]
        low_right = -toeplitz[:, 2] - kx_row * ky_row * diag_pair
        upper_row = jnp.concatenate([top_left, top_right], axis=1)
        lower_row = jnp.concatenate([low_left, low_right], axis=1)
        return jnp.where(lower_half == 1, lower_row, upper_row)
    return jax.vmap(one_row, out_axes=1)(window_rows)

def reference(labels):
    fields = field_stack(labels)
    spectra = jnp.fft.fft2(fields, axes=(1, 2))
    picks = (jnp.arange(KEEP) - (HARM - 1)) % NMAP
    picked = spectra[:, picks][:, :, picks] / float(NMAP * NMAP)
    coefficients = jnp.stack([jnp.real(picked), jnp.imag(picked)]).astype(jnp.float32)
    window_total = ROWS_DEV * N_SLAB
    spacing = ORDERS // (window_total // 2)
    all_rows = jnp.arange(window_total, dtype=jnp.int32).reshape(N_SLAB, ROWS_DEV)
    blocks = lax.map(lambda block_rows: build_rows(coefficients, block_rows, spacing), all_rows)
    return jnp.transpose(blocks, (1, 0, 2, 3)).reshape(2, window_total, 2 * ORDERS)
```

```python
import jax
import jax.numpy as jnp
import numpy as np
from jax import lax
from jax.experimental import pallas as pl
from jax.experimental.pallas import tpu as pltpu
from jax.sharding import PartitionSpec as P

NMAP = 2048
HARM = 101
ORDERS = HARM * HARM
ROWS_DEV = 64
SLABS = 16
ROWS = NMAP // SLABS
SPACING = ORDERS // (ROWS_DEV * SLABS // 2)
HALF = 104
MAPROWS = 2 * HALF
OWN = 40
EDGE = 8
TOP = 8
EXT = ROWS + 2 * EDGE
PERMITS = (1.0, 2.1, 4.0, 12.1)
MAPS = 3
NTAB = 112


def split_numpy(table):
    high = table.astype(jnp.bfloat16)
    low = (table - high.astype(np.float64)).astype(jnp.bfloat16)
    return high, low


def column_table():
    freq = np.arange(HARM)[:, None]
    angle = 2.0 * np.pi * (freq * np.arange(NMAP)[None, :] % NMAP) / NMAP
    table = np.zeros((MAPROWS, NMAP))
    table[:HARM] = np.cos(angle)
    table[HALF : HALF + HARM] = -np.sin(angle)
    return np.concatenate(split_numpy(table))


def row_table():
    freq = np.arange(HARM)[None, :]
    angle = 2.0 * np.pi * (freq * np.arange(NMAP)[:, None] % NMAP) / NMAP
    table = np.zeros((NMAP, 256))
    table[:, :HARM] = np.cos(angle)
    table[:, 128 : 128 + HARM] = np.sin(angle)
    return np.stack(split_numpy(table / float(NMAP * NMAP)))


def mirror_table():
    table = np.zeros((MAPROWS, 512), np.float32)
    for place in range(2 * HARM - 1):
        n = HARM - 1 - place
        table[abs(n), place] = 1.0
        table[HALF + abs(n), 256 + place] = np.sign(n)
    return table.astype(jnp.bfloat16)


def split(value):
    high = value.astype(jnp.bfloat16)
    low = (value - high.astype(jnp.float32)).astype(jnp.bfloat16)
    return high, low


def dot_f32(a, b, contract):
    return lax.dot_general(a, b, (contract, ((), ())), preferred_element_type=jnp.float32)


def by_label(labels, values):
    low = jnp.where(labels == 0, jnp.float32(values[0]), jnp.float32(values[1]))
    high = jnp.where(labels == 2, jnp.float32(values[2]), jnp.float32(values[3]))
    return jnp.where(labels < 2, low, high)


def spectrum_kernel(
    labels_ref, col_ref, row_ref, out_ref, ext, smooth_a, smooth_b, fields, spec, gathered,
    load_sem, edge_send, edge_recv, spec_send, spec_recv, own_send, own_recv,
):
    me = lax.axis_index("slab")
    before = lax.rem(me + SLABS - 1, SLABS)
    after = lax.rem(me + 1, SLABS)

    load = pltpu.make_async_copy(labels_ref, ext.at[pl.ds(EDGE, ROWS)], load_sem)
    load.start()

    barrier = pltpu.get_barrier_semaphore()
    for step in range(1, SLABS):
        pl.semaphore_signal(barrier, inc=1, device_id={"slab": lax.rem(me + step, SLABS)})
    pl.semaphore_wait(barrier, SLABS - 1)

    up = pltpu.make_async_remote_copy(
        labels_ref.at[pl.ds(0, EDGE)], ext.at[pl.ds(EDGE + ROWS, EDGE)],
        edge_send.at[0], edge_recv.at[0], device_id={"slab": before},
    )
    down = pltpu.make_async_remote_copy(
        labels_ref.at[pl.ds(ROWS - EDGE, EDGE)], ext.at[pl.ds(0, EDGE)],
        edge_send.at[1], edge_recv.at[1], device_id={"slab": after},
    )
    up.start()
    down.start()
    load.wait()
    up.wait()
    down.wait()

    def to_permit(i, carry):
        r = pl.multiple_of(8 * i, 8)
        smooth_a[pl.ds(TOP + r, 8), :] = by_label(ext[pl.ds(r, 8), :], PERMITS)
        return carry

    lax.fori_loop(0, EXT // 8, to_permit, 0)

    def shifted(ref, r, rows):
        prev = ref[pl.ds(r - 8, 8), :]
        mid = ref[pl.ds(r, rows), :]
        nxt = ref[pl.ds(r + rows, 8), :]
        up_ = jnp.concatenate([prev[7:], mid[:-1]], axis=0)
        down_ = jnp.concatenate([mid[1:], nxt[:1]], axis=0)
        return up_, mid, down_

    def smooth_once(src, dst):
        def body(i, carry):
            r = pl.multiple_of(TOP + 8 * i, 8)
            up_, mid, down_ = shifted(src, r, 8)
            side = pltpu.roll(mid, 1, 1) + pltpu.roll(mid, NMAP - 1, 1)
            dst[pl.ds(r, 8), :] = 0.5 * mid + 0.125 * (up_ + down_ + side)
            return carry

        lax.fori_loop(0, EXT // 8, body, 0)

    smooth_once(smooth_a, smooth_b)
    smooth_once(smooth_b, smooth_a)
    smooth_once(smooth_a, smooth_b)

    contrasts = [p - 1.0 / p for p in PERMITS]

    def make_fields(i, carry):
        r = pl.multiple_of(16 * i, 16)
        up_, mid, down_ = shifted(smooth_b, pl.multiple_of(TOP + EDGE + r, 8), 16)
        labels = ext[pl.ds(pl.multiple_of(EDGE + r, 8), 16), :]
        grad_x = 0.5 * (down_ - up_)
        grad_y = 0.5 * (pltpu.roll(mid, NMAP - 1, 1) - pltpu.roll(mid, 1, 1))
        permit = by_label(labels, PERMITS)
        factor = by_label(labels, contrasts) / (grad_x * grad_x + grad_y * grad_y + 1.0)
        along_x = factor * grad_x
        maps = (along_x * grad_y, permit - factor * grad_y * grad_y, along_x * grad_x - permit)
        for k in range(MAPS):
            high, low = split(maps[k])
            fields[k, 0, pl.ds(r, 16), :] = high
            fields[k, 1, pl.ds(r, 16), :] = low
        return carry

    lax.fori_loop(0, ROWS // 16, make_fields, 0)

    for k in range(MAPS):
        product = dot_f32(col_ref[...], fields[k].reshape(2 * ROWS, NMAP), ((1,), (1,)))
        half = product[:, :ROWS] + product[:, ROWS:]
        spec[MAPROWS * k : MAPROWS * (k + 1), :] = half[:MAPROWS] + half[MAPROWS:]
    spec[MAPROWS * MAPS :, :] = jnp.zeros((SLABS * OWN - MAPROWS * MAPS, ROWS), jnp.float32)

    def spec_copy(step):
        to = lax.rem(me + step, SLABS)
        return pltpu.make_async_remote_copy(
            spec.at[pl.ds(pl.multiple_of(to * OWN, 8), OWN)],
            gathered.at[:, pl.ds(pl.multiple_of(me * ROWS, 128), ROWS)],
            spec_send.at[step], spec_recv.at[step], device_id={"slab": to},
        )

    for step in range(1, SLABS):
        spec_copy(step).start()
    mine = pl.ds(pl.multiple_of(me * OWN, 8), OWN)
    gathered[:, pl.ds(pl.multiple_of(me * ROWS, 128), ROWS)] = spec[mine, :]
    for step in range(1, SLABS):
        spec_copy(step).wait()

    high, low = split(gathered[...])
    contract = ((1,), (0,))
    out_ref[mine, :] = (
        dot_f32(high, row_ref[0], contract) + dot_f32(low, row_ref[0], contract) + dot_f32(high, row_ref[1], contract)
    )

    def own_copy(step):
        to = lax.rem(me + step, SLABS)
        return pltpu.make_async_remote_copy(
            out_ref.at[mine], out_ref.at[mine], own_send.at[step], own_recv.at[step], device_id={"slab": to},
        )

    for step in range(1, SLABS):
        own_copy(step).start()
    for step in range(1, SLABS):
        own_copy(step).wait()


def spectrum(labels, col, row):
    vmem = pl.BlockSpec(memory_space=pltpu.VMEM)
    return pl.pallas_call(
        spectrum_kernel,
        out_shape=jax.ShapeDtypeStruct((SLABS * OWN, 256), jnp.float32),
        in_specs=[pl.BlockSpec(memory_space=pl.ANY), vmem, vmem],
        out_specs=vmem,
        scratch_shapes=[
            pltpu.VMEM((EXT, NMAP), jnp.int32),
            pltpu.VMEM((EXT + 2 * TOP, NMAP), jnp.float32),
            pltpu.VMEM((EXT + 2 * TOP, NMAP), jnp.float32),
            pltpu.VMEM((MAPS, 2, ROWS, NMAP), jnp.bfloat16),
            pltpu.VMEM((SLABS * OWN, ROWS), jnp.float32),
            pltpu.VMEM((OWN, NMAP), jnp.float32),
            pltpu.SemaphoreType.DMA,
            pltpu.SemaphoreType.DMA((2,)),
            pltpu.SemaphoreType.DMA((2,)),
            pltpu.SemaphoreType.DMA((SLABS,)),
            pltpu.SemaphoreType.DMA((SLABS,)),
            pltpu.SemaphoreType.DMA((SLABS,)),
            pltpu.SemaphoreType.DMA((SLABS,)),
        ],
        compiler_params=pltpu.CompilerParams(
            collective_id=0, has_side_effects=True, vmem_limit_bytes=40 * 1024 * 1024
        ),
        name="spectrum",
    )(labels, col, row)


def take_lanes(value, index):
    return jnp.take_along_axis(value, index, axis=1, mode="promise_in_bounds")


def build_kernel(me_ref, spec_ref, mirror_ref, out_ref, full, tab):
    group = pl.program_id(0)
    first_order = me_ref[0] * (ROWS_DEV // 2)
    p_last = (first_order + ROWS_DEV // 2 - 1) * SPACING // HARM
    tab_start = HARM - 2 - p_last

    @pl.when(group == 0)
    def make_table():
        mirror = mirror_ref[...]
        for k in range(MAPS):
            high, low = split(spec_ref[MAPROWS * k : MAPROWS * (k + 1), :].T)
            product = dot_f32(high, mirror, ((1,), (0,))) + dot_f32(low, mirror, ((1,), (0,)))
            cos_even, cos_odd = product[:128, :256], product[:128, 256:]
            sin_even, sin_odd = product[128:, :256], product[128:, 256:]
            full[0, k, 0] = cos_even + sin_odd
            full[0, k, 1] = cos_even - sin_odd
            full[1, k, 0] = cos_odd - sin_even
            full[1, k, 1] = cos_odd + sin_even
        odd = lax.broadcasted_iota(jnp.int32, (8, 256), 0) % 2 == 1

        def fill(i, carry):
            m = HARM - 1 - (tab_start + i)
            sign = jnp.where(m < 0, 1, 0)
            row = jnp.minimum(jnp.abs(m), 127)
            for part in range(2):
                rows = [jnp.broadcast_to(full[part, k, sign, pl.ds(row, 1), :], (8, 256)) for k in range(MAPS)]
                tab[part, 0, i] = jnp.where(odd, rows[2], rows[0])
                tab[part, 1, i] = jnp.where(odd, -rows[0], rows[1])
            return carry

        lax.fori_loop(0, HARM + 8, fill, 0)

    lane = lax.broadcasted_iota(jnp.int32, (8, 128), 1)
    sub = lax.broadcasted_iota(jnp.int32, (8, 128), 0)
    t0 = first_order + 4 * group
    p0 = t0 * SPACING // HARM
    order = (t0 + sub // 2) * SPACING
    cross = order >= (p0 + 1) * HARM
    cross_wide = jnp.concatenate([cross, cross], axis=1)
    p = jnp.where(cross, p0 + 1, p0)
    q = order - p * HARM
    offset = HARM - 1 - q
    base = lane + offset
    first = HARM - 1 - p0 - tab_start
    current = [None, None]
    for k in range(2 * HARM):
        half, p_j = k // HARM, k % HARM
        tile, start = divmod(HARM * k, 128)
        index = (base + (128 - start)) & 127
        in_low = index >= offset
        for part in range(2):
            source = jnp.where(cross_wide, tab[part, half, first + p_j - 1], tab[part, half, first + p_j])
            segment = jnp.where(in_low, take_lanes(source[:, :128], index), take_lanes(source[:, 128:], index))
            merged = segment if start == 0 else jnp.where(lane < start, current[part], segment)
            if start + HARM >= 128:
                out_ref[part, :, 128 * tile : 128 * tile + 128] = merged
                current[part] = segment
            else:
                current[part] = merged
    last = 2 * ORDERS // 128 * 128
    for part in range(2):
        out_ref[part, :, last:] = current[part][:, : 2 * ORDERS - last]

    upper = sub % 2 == 0
    kx = 0.3 + 0.02 * (p - HARM // 2).astype(jnp.float32)
    ky = 0.2 + 0.02 * (q - HARM // 2).astype(jnp.float32)
    for half in range(2):
        if half == 0:
            wave = jnp.where(upper, kx * ky, ky * ky)
        else:
            wave = -jnp.where(upper, kx * kx, kx * ky)
        column = (t0 * SPACING + half * ORDERS) // 128 * 128
        place = order + half * ORDERS - column
        for j in range(2):
            lanes = pl.ds(pl.multiple_of(column + 128 * j, 128), 128)
            out_ref[0, :, lanes] = out_ref[0, :, lanes] + jnp.where(place == lane + 128 * j, wave, 0.0)


def build(me, spec, mirror):
    return pl.pallas_call(
        build_kernel,
        out_shape=jax.ShapeDtypeStruct((2, ROWS_DEV, 2 * ORDERS), jnp.float32),
        grid_spec=pltpu.PrefetchScalarGridSpec(
            num_scalar_prefetch=1,
            grid=(ROWS_DEV // 8,),
            in_specs=[
                pl.BlockSpec((SLABS * OWN, 256), lambda g, m: (0, 0)),
                pl.BlockSpec((MAPROWS, 512), lambda g, m: (0, 0)),
            ],
            out_specs=pl.BlockSpec((2, 8, 2 * ORDERS), lambda g, m: (0, g, 0)),
            scratch_shapes=[
                pltpu.VMEM((2, MAPS, 2, 128, 256), jnp.float32),
                pltpu.VMEM((2, 2, NTAB, 8, 256), jnp.float32),
            ],
        ),
        compiler_params=pltpu.CompilerParams(vmem_limit_bytes=32 * 1024 * 1024),
        name="build",
    )(me, spec, mirror)


def shards(labels):
    me = lax.axis_index("slab").astype(jnp.int32).reshape(1)
    spec = spectrum(labels, jnp.asarray(column_table()), jnp.asarray(row_table()))
    return build(me, spec, jnp.asarray(mirror_table()))


def solution(mesh):
    return jax.shard_map(
        shards,
        mesh=mesh,
        in_specs=(P(("layer", "slab"), None),),
        out_specs=P(None, ("layer", "slab"), None),
        check_vma=False,
    )
```

```python
import jax
import jax.numpy as jnp
import numpy as np
from jax import lax
from jax.experimental import pallas as pl
from jax.experimental.pallas import tpu as pltpu
from jax.sharding import PartitionSpec as P

NMAP = 2048
HARM = 101
ORDERS = HARM * HARM
ROWS_DEV = 64
SLABS = 16
ROWS = NMAP // SLABS
SPACING = ORDERS // (ROWS_DEV * SLABS // 2)
HALF = 104
MAPROWS = 2 * HALF
OWN = 40
EDGE = 8
TOP = 8
EXT = ROWS + 2 * EDGE
PERMITS = (1.0, 2.1, 4.0, 12.1)
MAPS = 3
TABLE = 112
LEAD = 8
PITCH = 9
STRIPS = NMAP // 128
CHIPS = SLABS // 2
EARLY = 24


def split_numpy(table):
    high = table.astype(jnp.bfloat16)
    low = (table - high.astype(np.float64)).astype(jnp.bfloat16)
    return high, low


def column_table():
    freq = np.arange(HARM)[:, None]
    angle = 2.0 * np.pi * (freq * np.arange(NMAP)[None, :] % NMAP) / NMAP
    table = np.zeros((MAPROWS, NMAP))
    table[:HARM] = np.cos(angle)
    table[HALF : HALF + HARM] = -np.sin(angle)
    return np.concatenate(split_numpy(table))


def row_table():
    freq = np.arange(HARM)[None, :]
    angle = 2.0 * np.pi * (freq * np.arange(NMAP)[:, None] % NMAP) / NMAP
    table = np.zeros((NMAP, 256))
    table[:, :HARM] = np.cos(angle)
    table[:, 128 : 128 + HARM] = np.sin(angle)
    return np.stack(split_numpy(table / float(NMAP * NMAP)))


def split(value):
    high = value.astype(jnp.bfloat16)
    low = (value - high.astype(jnp.float32)).astype(jnp.bfloat16)
    return high, low


def dot_f32(a, b, contract):
    return lax.dot_general(a, b, (contract, ((), ())), preferred_element_type=jnp.float32)


def by_label(labels, values):
    low = jnp.where(labels == 0, jnp.float32(values[0]), jnp.float32(values[1]))
    high = jnp.where(labels == 2, jnp.float32(values[2]), jnp.float32(values[3]))
    return jnp.where(labels < 2, low, high)


def spectrum_kernel(
    labels_ref, col_hbm, row_hbm, out_ref, ext, smooth_a, smooth_b, fields, spec, gathered, col_ref, row_ref,
    load_sem, edge_send, edge_recv, spec_send, spec_recv, own_send, own_recv,
):
    me = lax.axis_index("slab")
    before = lax.rem(me + SLABS - 1, SLABS)
    after = lax.rem(me + 1, SLABS)

    load = pltpu.make_async_copy(labels_ref, ext.at[pl.ds(EDGE, ROWS)], load_sem.at[0])
    load.start()
    load_col = pltpu.make_async_copy(col_hbm, col_ref, load_sem.at[1])
    load_row = pltpu.make_async_copy(row_hbm, row_ref, load_sem.at[2])

    barrier = pltpu.get_barrier_semaphore()
    for step in range(1, SLABS):
        pl.semaphore_signal(barrier, inc=1, device_id={"slab": lax.rem(me + step, SLABS)})
    pl.semaphore_wait(barrier, SLABS - 1)

    up = pltpu.make_async_remote_copy(
        labels_ref.at[pl.ds(0, EDGE)], ext.at[pl.ds(EDGE + ROWS, EDGE)],
        edge_send.at[0], edge_recv.at[0], device_id={"slab": before},
    )
    down = pltpu.make_async_remote_copy(
        labels_ref.at[pl.ds(ROWS - EDGE, EDGE)], ext.at[pl.ds(0, EDGE)],
        edge_send.at[1], edge_recv.at[1], device_id={"slab": after},
    )
    up.start()
    down.start()
    load_col.start()
    load_row.start()

    def over_tiles(body, count, skip_at=None, skip=0, first=0):
        def step(i, carry):
            body(first + i if skip_at is None else first + i + jnp.where(i >= skip_at, skip, 0))
            return carry

        lax.fori_loop(0, count, step, 0)

    def to_permit(tile):
        r = pl.multiple_of(8 * tile, 8)
        for j in range(STRIPS):
            smooth_a[j, pl.ds(TOP + r, 8), :] = by_label(ext[pl.ds(r, 8), 128 * j : 128 * (j + 1)], PERMITS)

    def sides(mid, rows):
        lane = lax.broadcasted_iota(jnp.int32, (STRIPS, rows, 128), 2)
        flat = mid.reshape(STRIPS * rows, 128)
        ahead = pltpu.roll(flat, 127, 1).reshape(STRIPS, rows, 128)
        behind = pltpu.roll(flat, 1, 1).reshape(STRIPS, rows, 128)
        ahead = jnp.where(lane == 127, jnp.concatenate([ahead[1:], ahead[:1]], axis=0), ahead)
        behind = jnp.where(lane == 0, jnp.concatenate([behind[-1:], behind[:-1]], axis=0), behind)
        return behind, ahead

    def smooth_tile(src, dst):
        def body(tile):
            r = pl.multiple_of(TOP + 8 * tile, 8)
            mid = src[:, pl.ds(r, 8), :]
            behind, ahead = sides(mid, 8)
            around = src[:, pl.ds(r - 1, 8), :] + src[:, pl.ds(r + 1, 8), :] + behind + ahead
            dst[:, pl.ds(r, 8), :] = 0.5 * mid + 0.125 * around

        return body

    contrasts = [p - 1.0 / p for p in PERMITS]

    def make_fields(block):
        r = pl.multiple_of(16 * block, 16)
        at = pl.multiple_of(TOP + EDGE + r, 8)
        behind, ahead = sides(smooth_b[:, pl.ds(at, 16), :], 16)
        grad_x = 0.5 * (smooth_b[:, pl.ds(at + 1, 16), :] - smooth_b[:, pl.ds(at - 1, 16), :])
        grad_y = 0.5 * (ahead - behind)
        for j in range(STRIPS):
            lanes = slice(128 * j, 128 * (j + 1))
            labels = ext[pl.ds(pl.multiple_of(EDGE + r, 8), 16), lanes]
            permit = by_label(labels, PERMITS)
            gx, gy = grad_x[j], grad_y[j]
            factor = by_label(labels, contrasts) / (gx * gx + gy * gy + 1.0)
            along_x = factor * gx
            maps = (along_x * gy, permit - factor * gy * gy, along_x * gx - permit)
            for k in range(MAPS):
                high, low = split(maps[k])
                fields[k, 0, pl.ds(r, 16), lanes] = high
                fields[k, 1, pl.ds(r, 16), lanes] = low

    load.wait()
    over_tiles(to_permit, 16, first=1)
    over_tiles(smooth_tile(smooth_a, smooth_b), 14, first=2)
    over_tiles(smooth_tile(smooth_b, smooth_a), 12, first=3)
    over_tiles(smooth_tile(smooth_a, smooth_b), 10, first=4)
    over_tiles(make_fields, 4, first=2)
    up.wait()
    down.wait()
    over_tiles(to_permit, 2, 1, 16)
    over_tiles(smooth_tile(smooth_a, smooth_b), 4, 2, 14)
    over_tiles(smooth_tile(smooth_b, smooth_a), 6, 3, 12)
    over_tiles(smooth_tile(smooth_a, smooth_b), 8, 4, 10)
    over_tiles(make_fields, 4, 2, 4)

    load_col.wait()
    for k in range(MAPS):
        product = dot_f32(col_ref[...], fields[k].reshape(2 * ROWS, NMAP), ((1,), (1,)))
        half = product[:, :ROWS] + product[:, ROWS:]
        spec[MAPROWS * k : MAPROWS * (k + 1), :] = half[:MAPROWS] + half[MAPROWS:]
    spec[MAPROWS * MAPS :, :] = jnp.zeros((SLABS * OWN - MAPROWS * MAPS, ROWS), jnp.float32)

    def spec_copy(step):
        to = lax.rem(me + step, SLABS)
        return pltpu.make_async_remote_copy(
            spec.at[pl.ds(pl.multiple_of(to * OWN, 8), OWN)],
            gathered.at[:, pl.ds(pl.multiple_of(me * ROWS, 128), ROWS)],
            spec_send.at[step], spec_recv.at[step], device_id={"slab": to},
        )

    for step in range(1, SLABS):
        spec_copy(step).start()
    mine = pl.ds(pl.multiple_of(me * OWN, 8), OWN)
    gathered[:, pl.ds(pl.multiple_of(me * ROWS, 128), ROWS)] = spec[mine, :]
    load_row.wait()
    for step in range(1, SLABS):
        spec_copy(step).wait()

    high, low = split(gathered[...])
    contract = ((1,), (0,))
    out_ref[mine, :] = (
        dot_f32(high, row_ref[0], contract) + dot_f32(low, row_ref[0], contract) + dot_f32(high, row_ref[1], contract)
    )

    core = lax.rem(me, 2)
    chip = lax.div(me, 2)

    def ship(slot, origin, to, sibling=False, first=0, count=OWN):
        start = (2 * lax.rem(chip + origin + CHIPS, CHIPS) + core) * OWN + first
        rows = out_ref.at[pl.ds(pl.multiple_of(start, 8), count)]
        target = me + 1 - 2 * core if sibling else 2 * lax.rem(chip + to + CHIPS, CHIPS) + core
        return pltpu.make_async_remote_copy(
            rows, rows, own_send.at[slot], own_recv.at[slot], device_id={"slab": target}
        )

    up_part, down_part = dict(first=0, count=EARLY), dict(first=EARLY, count=OWN - EARLY)
    chips = [ship(0, 0, 2), ship(1, 0, -2), ship(2, 0, 1), ship(3, 0, -1),
             ship(4, -2, 2, **up_part), ship(5, 2, -2, **down_part), ship(6, -2, 1), ship(7, 2, -1)]
    siblings = [ship(8, -2, 0, True), ship(9, 2, 0, True), ship(10, -1, 0, True), ship(11, 1, 0, True),
                ship(12, 4, 0, True, **up_part), ship(13, 4, 0, True, **down_part),
                ship(14, -3, 0, True), ship(15, 3, 0, True), ship(16, 0, 0, True)]
    for i in range(4):
        chips[i].start()
    siblings[8].start()
    for i in range(2):
        chips[i].wait_recv()
        chips[4 + i].start()
        chips[6 + i].start()
        siblings[i].start()
    for i in range(2, 8):
        chips[i].wait_recv()
        siblings[i].start()
    for copy in chips:
        copy.wait_send()
    for copy in siblings:
        copy.wait()


def spectrum(labels, col, row):
    vmem = pl.BlockSpec(memory_space=pltpu.VMEM)
    hbm = pl.BlockSpec(memory_space=pltpu.HBM)
    return pl.pallas_call(
        spectrum_kernel,
        out_shape=jax.ShapeDtypeStruct((SLABS * OWN, 256), jnp.float32),
        in_specs=[hbm, hbm, hbm],
        out_specs=vmem,
        scratch_shapes=[
            pltpu.VMEM((EXT, NMAP), jnp.int32),
            pltpu.VMEM((STRIPS, EXT + 2 * TOP, 128), jnp.float32),
            pltpu.VMEM((STRIPS, EXT + 2 * TOP, 128), jnp.float32),
            pltpu.VMEM((MAPS, 2, ROWS, NMAP), jnp.bfloat16),
            pltpu.VMEM((SLABS * OWN, ROWS), jnp.float32),
            pltpu.VMEM((OWN, NMAP), jnp.float32),
            pltpu.VMEM((2 * MAPROWS, NMAP), jnp.bfloat16),
            pltpu.VMEM((2, NMAP, 256), jnp.bfloat16),
            pltpu.SemaphoreType.DMA((3,)),
            pltpu.SemaphoreType.DMA((2,)),
            pltpu.SemaphoreType.DMA((2,)),
            pltpu.SemaphoreType.DMA((SLABS,)),
            pltpu.SemaphoreType.DMA((SLABS,)),
            pltpu.SemaphoreType.DMA((17,)),
            pltpu.SemaphoreType.DMA((17,)),
        ],
        compiler_params=pltpu.CompilerParams(
            collective_id=0, has_side_effects=True, vmem_limit_bytes=63 * 1024 * 1024
        ),
        name="spectrum",
    )(labels, col, row)


def sign_of(value):
    return jnp.where(value > 0, 1.0, jnp.where(value < 0, -1.0, 0.0))


def build_kernel(me_ref, spec_ref, out_ref, toeplitz, windows):
    group = pl.program_id(0)
    first_order = me_ref[0] * (ROWS_DEV // 2)
    p_last = (first_order + ROWS_DEV // 2 - 1) * SPACING // HARM

    @pl.when(group == 0)
    def make_table():
        row = lax.broadcasted_iota(jnp.int32, (2 * TABLE, 256), 0)
        lane = lax.broadcasted_iota(jnp.int32, (2 * TABLE, 256), 1)
        m = p_last - jnp.where(row < TABLE, row, row - TABLE)
        from_cos = jnp.where(lane == jnp.abs(m), 1.0, 0.0)
        from_sin = jnp.where(lane == 128 + jnp.abs(m), sign_of(m), 0.0)
        pick = jnp.where(row < TABLE, from_cos, from_sin).astype(jnp.bfloat16)
        row = lax.broadcasted_iota(jnp.int32, (MAPROWS, 512), 0)
        lane = lax.broadcasted_iota(jnp.int32, (MAPROWS, 512), 1)
        n = HARM - 1 - (lane & 255)
        size = jnp.where(n >= 1 - HARM, jnp.abs(n), MAPROWS)
        even = jnp.where(row == size, 1.0, 0.0)
        uneven = jnp.where(row - HALF == size, sign_of(n), 0.0)
        mirror = jnp.where(lane < 256, even, uneven).astype(jnp.bfloat16)
        for k in range(MAPS):
            high, low = split(spec_ref[MAPROWS * k : MAPROWS * (k + 1), :])
            high, low = split(dot_f32(pick, high, ((1,), (1,))) + dot_f32(pick, low, ((1,), (1,))))
            product = dot_f32(high, mirror, ((1,), (0,))) + dot_f32(low, mirror, ((1,), (0,)))
            cos_rows, sin_rows = product[:TABLE], product[TABLE:]
            real = cos_rows[:, :256] + sin_rows[:, 256:]
            imag = cos_rows[:, 256:] - sin_rows[:, :256]
            for part, value in enumerate((real, imag)):
                rows = pl.ds((part * MAPS + k) * TABLE, TABLE)
                toeplitz[rows, :256], toeplitz[rows, 256:] = split(value)

    t0 = first_order + 4 * group
    row = lax.broadcasted_iota(jnp.int32, (512, 256), 0) & 255
    lane = lax.broadcasted_iota(jnp.int32, (512, 256), 1)
    for pair in range(2):
        orders = [(t0 + 2 * pair + j) * SPACING for j in range(2)]
        p_pair = [order // HARM for order in orders]
        q_pair = [order - p * HARM for order, p in zip(orders, p_pair)]
        source = jnp.where(lane < 128, lane - q_pair[0], lane - 128 - q_pair[1]) + HARM - 1
        shift = jnp.where(row == source, 1.0, 0.0).astype(jnp.bfloat16)
        moved = dot_f32(toeplitz[...], shift, ((1,), (0,)))
        for j in range(2):
            top = (LEAD - (p_last - p_pair[j])) * PITCH + 4 * pair + 2 * j
            for part in range(2):
                cross_xy, right_up, left_low = (
                    moved[(part * MAPS + k) * TABLE : (part * MAPS + k + 1) * TABLE, 128 * j : 128 * j + 128]
                    for k in range(MAPS)
                )
                upper = pl.ds(top, TABLE, stride=PITCH)
                lower = pl.ds(top + 1, TABLE, stride=PITCH)
                windows[part, 0, upper, :] = cross_xy
                windows[part, 0, lower, :] = left_low
                windows[part, 1, upper, :] = right_up
                windows[part, 1, lower, :] = -cross_xy

    lane = lax.broadcasted_iota(jnp.int32, (8, 128), 1)
    sub = lax.broadcasted_iota(jnp.int32, (8, 128), 0)
    current = [None, None]
    for k in range(2 * HARM):
        half, p_j = divmod(k, HARM)
        tile, start = divmod(HARM * k, 128)
        for part in range(2):
            segment = windows[part, half, (LEAD + p_j) * PITCH : (LEAD + p_j) * PITCH + 8, :]
            if start:
                segment = pltpu.roll(segment, start, 1)
                merged = jnp.where(lane < start, current[part], segment)
            else:
                merged = segment
            if start + HARM >= 128:
                out_ref[part, :, 128 * tile : 128 * tile + 128] = merged
                current[part] = segment
            else:
                current[part] = merged
    last = 2 * ORDERS // 128 * 128
    for part in range(2):
        out_ref[part, :, last:] = current[part][:, : 2 * ORDERS - last]

    order = (t0 + sub // 2) * SPACING
    p0 = t0 * SPACING // HARM
    p = jnp.where(order >= (p0 + 1) * HARM, p0 + 1, p0)
    q = order - p * HARM
    upper = sub % 2 == 0
    kx = 0.3 + 0.02 * (p - HARM // 2).astype(jnp.float32)
    ky = 0.2 + 0.02 * (q - HARM // 2).astype(jnp.float32)
    for half in range(2):
        if half == 0:
            wave = jnp.where(upper, kx * ky, ky * ky)
        else:
            wave = -jnp.where(upper, kx * kx, kx * ky)
        column = (t0 * SPACING + half * ORDERS) // 128 * 128
        place = order + half * ORDERS - column
        for j in range(2):
            lanes = pl.ds(pl.multiple_of(column + 128 * j, 128), 128)
            out_ref[0, :, lanes] = out_ref[0, :, lanes] + jnp.where(place == lane + 128 * j, wave, 0.0)


def build(me, spec):
    return pl.pallas_call(
        build_kernel,
        out_shape=jax.ShapeDtypeStruct((2, ROWS_DEV, 2 * ORDERS), jnp.float32),
        grid_spec=pltpu.PrefetchScalarGridSpec(
            num_scalar_prefetch=1,
            grid=(ROWS_DEV // 8,),
            in_specs=[pl.BlockSpec((SLABS * OWN, 256), lambda g, m: (0, 0))],
            out_specs=pl.BlockSpec((2, 8, 2 * ORDERS), lambda g, m: (0, g, 0)),
            scratch_shapes=[
                pltpu.VMEM((2 * MAPS * TABLE, 512), jnp.bfloat16),
                pltpu.VMEM((2, 2, (LEAD + TABLE) * PITCH, 128), jnp.float32),
            ],
        ),
        compiler_params=pltpu.CompilerParams(vmem_limit_bytes=63 * 1024 * 1024),
        name="build",
    )(me, spec)


def shards(labels):
    me = lax.axis_index("slab").astype(jnp.int32).reshape(1)
    spec = spectrum(labels, jnp.asarray(column_table()), jnp.asarray(row_table()))
    return build(me, spec)


def solution(mesh):
    return jax.shard_map(
        shards,
        mesh=mesh,
        in_specs=(P(("layer", "slab"), None),),
        out_specs=P(None, ("layer", "slab"), None),
        check_vma=False,
    )
```

```python
import jax
import jax.numpy as jnp
import numpy as np
from jax import lax
from jax.experimental import pallas as pl
from jax.experimental.pallas import tpu as pltpu
from jax.sharding import PartitionSpec as P

NMAP = 2048
HARM = 101
ORDERS = HARM * HARM
ROWS_DEV = 64
SLABS = 16
ROWS = NMAP // SLABS
SPACING = ORDERS // (ROWS_DEV * SLABS // 2)
HALF = 104
MAPROWS = 2 * HALF
OWN = 40
EDGE = 8
TOP = 8
EXT = ROWS + 2 * EDGE
PERMITS = (1.0, 2.1, 4.0, 12.1)
MAPS = 3
TABLE = 112
LEAD = 8
PITCH = 9
STRIPS = NMAP // 128
GROUPS = ROWS_DEV // 8
SLOTS = 4
CHIPS = SLABS // 2
PHASES = ((0, 0, 24), (SLABS * 24, 24, 16))


def split_numpy(table):
    high = table.astype(jnp.bfloat16)
    low = (table - high.astype(np.float64)).astype(jnp.bfloat16)
    return high, low


def column_table():
    freq = np.arange(HARM)[:, None]
    angle = 2.0 * np.pi * (freq * np.arange(NMAP)[None, :] % NMAP) / NMAP
    table = np.zeros((MAPROWS, NMAP))
    table[:HARM] = np.cos(angle)
    table[HALF : HALF + HARM] = -np.sin(angle)
    return np.concatenate(split_numpy(table))


def row_table():
    freq = np.arange(HARM)[None, :]
    angle = 2.0 * np.pi * (freq * np.arange(NMAP)[:, None] % NMAP) / NMAP
    table = np.zeros((NMAP, 256))
    table[:, :HARM] = np.cos(angle)
    table[:, 128 : 128 + HARM] = np.sin(angle)
    return np.stack(split_numpy(table / float(NMAP * NMAP)))


def split(value):
    high = value.astype(jnp.bfloat16)
    low = (value - high.astype(jnp.float32)).astype(jnp.bfloat16)
    return high, low


def dot_f32(a, b, contract):
    return lax.dot_general(a, b, (contract, ((), ())), preferred_element_type=jnp.float32)


def by_label(labels, values):
    low = jnp.where(labels == 0, jnp.float32(values[0]), jnp.float32(values[1]))
    high = jnp.where(labels == 2, jnp.float32(values[2]), jnp.float32(values[3]))
    return jnp.where(labels < 2, low, high)


def spectrum_kernel(
    labels_ref, col_hbm, row_hbm, out_ref, ext, smooth_a, smooth_b, fields, spec, gathered, col_ref, row_ref,
    load_sem, edge_send, edge_recv, spec_send, spec_recv, own_send, own_recv,
):
    me = lax.axis_index("slab")
    before = lax.rem(me + SLABS - 1, SLABS)
    after = lax.rem(me + 1, SLABS)

    load = pltpu.make_async_copy(labels_ref, ext.at[pl.ds(EDGE, ROWS)], load_sem.at[0])
    load.start()
    load_col = pltpu.make_async_copy(col_hbm, col_ref, load_sem.at[1])
    load_row = pltpu.make_async_copy(row_hbm, row_ref, load_sem.at[2])

    barrier = pltpu.get_barrier_semaphore()
    for step in range(1, SLABS):
        pl.semaphore_signal(barrier, inc=1, device_id={"slab": lax.rem(me + step, SLABS)})
    pl.semaphore_wait(barrier, SLABS - 1)

    up = pltpu.make_async_remote_copy(
        labels_ref.at[pl.ds(0, EDGE)], ext.at[pl.ds(EDGE + ROWS, EDGE)],
        edge_send.at[0], edge_recv.at[0], device_id={"slab": before},
    )
    down = pltpu.make_async_remote_copy(
        labels_ref.at[pl.ds(ROWS - EDGE, EDGE)], ext.at[pl.ds(0, EDGE)],
        edge_send.at[1], edge_recv.at[1], device_id={"slab": after},
    )
    up.start()
    down.start()
    load_col.start()
    load_row.start()

    def over_tiles(body, count, skip_at=None, skip=0, first=0):
        def step(i, carry):
            body(first + i if skip_at is None else first + i + jnp.where(i >= skip_at, skip, 0))
            return carry

        lax.fori_loop(0, count, step, 0)

    def to_permit(tile):
        r = pl.multiple_of(8 * tile, 8)
        for j in range(STRIPS):
            smooth_a[j, pl.ds(TOP + r, 8), :] = by_label(ext[pl.ds(r, 8), 128 * j : 128 * (j + 1)], PERMITS)

    def sides(mid, rows):
        lane = lax.broadcasted_iota(jnp.int32, (STRIPS, rows, 128), 2)
        flat = mid.reshape(STRIPS * rows, 128)
        ahead = pltpu.roll(flat, 127, 1).reshape(STRIPS, rows, 128)
        behind = pltpu.roll(flat, 1, 1).reshape(STRIPS, rows, 128)
        ahead = jnp.where(lane == 127, jnp.concatenate([ahead[1:], ahead[:1]], axis=0), ahead)
        behind = jnp.where(lane == 0, jnp.concatenate([behind[-1:], behind[:-1]], axis=0), behind)
        return behind, ahead

    def smooth_tile(src, dst):
        def body(tile):
            r = pl.multiple_of(TOP + 8 * tile, 8)
            mid = src[:, pl.ds(r, 8), :]
            behind, ahead = sides(mid, 8)
            around = src[:, pl.ds(r - 1, 8), :] + src[:, pl.ds(r + 1, 8), :] + behind + ahead
            dst[:, pl.ds(r, 8), :] = 0.5 * mid + 0.125 * around

        return body

    contrasts = [p - 1.0 / p for p in PERMITS]

    def make_fields(block):
        r = pl.multiple_of(16 * block, 16)
        at = pl.multiple_of(TOP + EDGE + r, 8)
        behind, ahead = sides(smooth_b[:, pl.ds(at, 16), :], 16)
        grad_x = 0.5 * (smooth_b[:, pl.ds(at + 1, 16), :] - smooth_b[:, pl.ds(at - 1, 16), :])
        grad_y = 0.5 * (ahead - behind)
        for j in range(STRIPS):
            lanes = slice(128 * j, 128 * (j + 1))
            labels = ext[pl.ds(pl.multiple_of(EDGE + r, 8), 16), lanes]
            permit = by_label(labels, PERMITS)
            gx, gy = grad_x[j], grad_y[j]
            factor = by_label(labels, contrasts) / (gx * gx + gy * gy + 1.0)
            along_x = factor * gx
            maps = (along_x * gy, permit - factor * gy * gy, along_x * gx - permit)
            for k in range(MAPS):
                high, low = split(maps[k])
                fields[k, 0, pl.ds(r, 16), lanes] = high
                fields[k, 1, pl.ds(r, 16), lanes] = low

    load.wait()
    over_tiles(to_permit, 16, first=1)
    over_tiles(smooth_tile(smooth_a, smooth_b), 14, first=2)
    over_tiles(smooth_tile(smooth_b, smooth_a), 12, first=3)
    over_tiles(smooth_tile(smooth_a, smooth_b), 10, first=4)
    over_tiles(make_fields, 4, first=2)
    up.wait()
    down.wait()
    over_tiles(to_permit, 2, 1, 16)
    over_tiles(smooth_tile(smooth_a, smooth_b), 4, 2, 14)
    over_tiles(smooth_tile(smooth_b, smooth_a), 6, 3, 12)
    over_tiles(smooth_tile(smooth_a, smooth_b), 8, 4, 10)
    over_tiles(make_fields, 4, 2, 4)

    def spec_copy(phase, step):
        to = lax.rem(me + step, SLABS)
        base, first, count = PHASES[phase]
        return pltpu.make_async_remote_copy(
            spec.at[pl.ds(pl.multiple_of(base + to * count, 8), count)],
            gathered.at[pl.ds(first, count), pl.ds(pl.multiple_of(me * ROWS, 128), ROWS)],
            spec_send.at[phase, step], spec_recv.at[phase, step], device_id={"slab": to},
        )

    def send_spec(phase):
        for step in range(1, SLABS):
            spec_copy(phase, step).start()
        base, first, count = PHASES[phase]
        mine = spec[pl.ds(pl.multiple_of(base + me * count, 8), count), :]
        gathered[first : first + count, pl.ds(pl.multiple_of(me * ROWS, 128), ROWS)] = mine

    load_col.wait()
    spec[MAPROWS * MAPS :, :] = jnp.zeros((SLABS * OWN - MAPROWS * MAPS, ROWS), jnp.float32)
    for k in range(MAPS):
        product = dot_f32(col_ref[...], fields[k].reshape(2 * ROWS, NMAP), ((1,), (1,)))
        half = product[:, :ROWS] + product[:, ROWS:]
        spec[MAPROWS * k : MAPROWS * (k + 1), :] = half[:MAPROWS] + half[MAPROWS:]
        if k > 0:
            send_spec(k - 1)

    core = lax.rem(me, 2)
    chip = lax.div(me, 2)

    def own_copies(phase):
        base, _, count = PHASES[phase]

        def ship(slot, origin, to, sibling=False, first=0, size=count):
            start = base + (2 * lax.rem(chip + origin + CHIPS, CHIPS) + core) * count + first
            rows = out_ref.at[pl.ds(pl.multiple_of(start, 8), size)]
            target = me + 1 - 2 * core if sibling else 2 * lax.rem(chip + to + CHIPS, CHIPS) + core
            return pltpu.make_async_remote_copy(
                rows, rows, own_send.at[phase, slot], own_recv.at[phase, slot], device_id={"slab": target}
            )

        up_part, down_part = dict(first=0, size=count - 8), dict(first=count - 8, size=8)
        chips = [ship(0, 0, 2), ship(1, 0, -2), ship(2, 0, 1), ship(3, 0, -1),
                 ship(4, -2, 2, **up_part), ship(5, 2, -2, **down_part), ship(6, -2, 1), ship(7, 2, -1)]
        siblings = [ship(8, -2, 0, True), ship(9, 2, 0, True), ship(10, -1, 0, True), ship(11, 1, 0, True),
                    ship(12, 4, 0, True, **up_part), ship(13, 4, 0, True, **down_part),
                    ship(14, -3, 0, True), ship(15, 3, 0, True), ship(16, 0, 0, True)]
        return chips, siblings

    load_row.wait()
    contract = ((1,), (0,))
    chips, siblings = zip(*(own_copies(phase) for phase in range(2)))
    for phase, (base, first, count) in enumerate(PHASES):
        for step in range(1, SLABS):
            spec_copy(phase, step).wait_recv()
        high, low = split(gathered[first : first + count, :])
        out_ref[pl.ds(pl.multiple_of(base + me * count, 8), count), :] = (
            dot_f32(high, row_ref[0], contract) + dot_f32(low, row_ref[0], contract) + dot_f32(high, row_ref[1], contract)
        )
        for i in range(4):
            chips[phase][i].start()
        siblings[phase][8].start()
    for phase in range(2):
        for i in range(2):
            chips[phase][i].wait_recv()
            chips[phase][4 + i].start()
            chips[phase][6 + i].start()
            siblings[phase][i].start()
        for i in range(2, 4):
            chips[phase][i].wait_recv()
            siblings[phase][i].start()
    for phase in range(2):
        for i in range(4, 8):
            chips[phase][i].wait_recv()
            siblings[phase][i].start()
    for phase in range(2):
        for step in range(1, SLABS):
            spec_copy(phase, step).wait_send()
        for copy in chips[phase]:
            copy.wait_send()
        for copy in siblings[phase]:
            copy.wait()


def spectrum(labels, col, row):
    vmem = pl.BlockSpec(memory_space=pltpu.VMEM)
    hbm = pl.BlockSpec(memory_space=pltpu.HBM)
    return pl.pallas_call(
        spectrum_kernel,
        out_shape=jax.ShapeDtypeStruct((SLABS * OWN, 256), jnp.float32),
        in_specs=[hbm, hbm, hbm],
        out_specs=vmem,
        scratch_shapes=[
            pltpu.VMEM((EXT, NMAP), jnp.int32),
            pltpu.VMEM((STRIPS, EXT + 2 * TOP, 128), jnp.float32),
            pltpu.VMEM((STRIPS, EXT + 2 * TOP, 128), jnp.float32),
            pltpu.VMEM((MAPS, 2, ROWS, NMAP), jnp.bfloat16),
            pltpu.VMEM((SLABS * OWN, ROWS), jnp.float32),
            pltpu.VMEM((OWN, NMAP), jnp.float32),
            pltpu.VMEM((2 * MAPROWS, NMAP), jnp.bfloat16),
            pltpu.VMEM((2, NMAP, 256), jnp.bfloat16),
            pltpu.SemaphoreType.DMA((3,)),
            pltpu.SemaphoreType.DMA((2,)),
            pltpu.SemaphoreType.DMA((2,)),
            pltpu.SemaphoreType.DMA((2, SLABS)),
            pltpu.SemaphoreType.DMA((2, SLABS)),
            pltpu.SemaphoreType.DMA((2, 17)),
            pltpu.SemaphoreType.DMA((2, 17)),
        ],
        compiler_params=pltpu.CompilerParams(
            collective_id=0, has_side_effects=True, vmem_limit_bytes=54016 * 1024
        ),
        name="spectrum",
    )(labels, col, row)


def sign_of(value):
    return jnp.where(value > 0, 1.0, jnp.where(value < 0, -1.0, 0.0))


def build_kernel(spec_ref, out_ref, toeplitz, windows_a, windows_b, stage, sem):
    first_order = lax.axis_index("slab") * (ROWS_DEV // 2)
    p_last = (first_order + ROWS_DEV // 2 - 1) * SPACING // HARM

    row = lax.broadcasted_iota(jnp.int32, (2 * TABLE, 256), 0)
    lane = lax.broadcasted_iota(jnp.int32, (2 * TABLE, 256), 1)
    m = p_last - jnp.where(row < TABLE, row, row - TABLE)
    from_cos = jnp.where(lane == jnp.abs(m), 1.0, 0.0)
    from_sin = jnp.where(lane == 128 + jnp.abs(m), sign_of(m), 0.0)
    pick = jnp.where(row < TABLE, from_cos, from_sin).astype(jnp.bfloat16)
    row = lax.broadcasted_iota(jnp.int32, (MAPROWS, 512), 0)
    lane = lax.broadcasted_iota(jnp.int32, (MAPROWS, 512), 1)
    n = HARM - 1 - (lane & 255)
    size = jnp.where(n >= 1 - HARM, jnp.abs(n), MAPROWS)
    even = jnp.where(row == size, 1.0, 0.0)
    uneven = jnp.where(row - HALF == size, sign_of(n), 0.0)
    mirror = jnp.where(lane < 256, even, uneven).astype(jnp.bfloat16)
    for k in range(MAPS):
        high, low = split(spec_ref[MAPROWS * k : MAPROWS * (k + 1), :])
        high, low = split(dot_f32(pick, high, ((1,), (1,))) + dot_f32(pick, low, ((1,), (1,))))
        product = dot_f32(high, mirror, ((1,), (0,))) + dot_f32(low, mirror, ((1,), (0,)))
        cos_rows, sin_rows = product[:TABLE], product[TABLE:]
        real = cos_rows[:, :256] + sin_rows[:, 256:]
        imag = cos_rows[:, 256:] - sin_rows[:, :256]
        for part, value in enumerate((real, imag)):
            rows = pl.ds((part * MAPS + k) * TABLE, TABLE)
            toeplitz[rows, :256], toeplitz[rows, 256:] = split(value)

    def shift_pair(group, pair):
        row = lax.broadcasted_iota(jnp.int32, (256, 256), 0)
        lane = lax.broadcasted_iota(jnp.int32, (256, 256), 1)
        orders = [(first_order + 4 * group + 2 * pair + j) * SPACING for j in range(2)]
        p_pair = [order // HARM for order in orders]
        q_pair = [order - p * HARM for order, p in zip(orders, p_pair)]
        source = jnp.where(lane < 128, lane - q_pair[0], lane - 128 - q_pair[1]) + HARM - 1
        shift = jnp.where(row == source, 1.0, 0.0).astype(jnp.bfloat16)
        shift = jnp.concatenate([shift, shift], axis=0)
        return p_pair, shift

    def make_windows(windows, p_pair, shift, pair, part):
        moved = dot_f32(toeplitz[part * MAPS * TABLE : (part + 1) * MAPS * TABLE, :], shift, ((1,), (0,)))
        for j in range(2):
            top = (LEAD - (p_last - p_pair[j])) * PITCH + 4 * pair + 2 * j
            cross_xy, right_up, left_low = (
                moved[k * TABLE : (k + 1) * TABLE, 128 * j : 128 * j + 128] for k in range(MAPS)
            )
            upper = pl.ds(top, TABLE, stride=PITCH)
            lower = pl.ds(top + 1, TABLE, stride=PITCH)
            windows[part, 0, upper, :] = cross_xy
            windows[part, 0, lower, :] = left_low
            windows[part, 1, upper, :] = right_up
            windows[part, 1, lower, :] = -cross_xy

    lane = lax.broadcasted_iota(jnp.int32, (8, 128), 1)
    sub = lax.broadcasted_iota(jnp.int32, (8, 128), 0)

    def emit(windows, slot, part, current, segments):
        for k in segments:
            half, p_j = divmod(k, HARM)
            tile, start = divmod(HARM * k, 128)
            segment = windows[part, half, (LEAD + p_j) * PITCH : (LEAD + p_j) * PITCH + 8, :]
            if start:
                segment = pltpu.roll(segment, start, 1)
                merged = jnp.where(lane < start, current, segment)
            else:
                merged = segment
            if start + HARM >= 128:
                stage[slot, part, :, 128 * tile : 128 * tile + 128] = merged
                current = segment
            else:
                current = merged
        if segments[-1] == 2 * HARM - 1:
            last = 2 * ORDERS // 128 * 128
            stage[slot, part, :, last:] = current[:, : 2 * ORDERS - last]
        return current

    def add_waves(group, slot):
        t0 = first_order + 4 * group
        order = (t0 + sub // 2) * SPACING
        p0 = t0 * SPACING // HARM
        p = jnp.where(order >= (p0 + 1) * HARM, p0 + 1, p0)
        q = order - p * HARM
        upper = sub % 2 == 0
        kx = 0.3 + 0.02 * (p - HARM // 2).astype(jnp.float32)
        ky = 0.2 + 0.02 * (q - HARM // 2).astype(jnp.float32)
        for half in range(2):
            if half == 0:
                wave = jnp.where(upper, kx * ky, ky * ky)
            else:
                wave = -jnp.where(upper, kx * kx, kx * ky)
            column = (t0 * SPACING + half * ORDERS) // 128 * 128
            place = order + half * ORDERS - column
            for j in range(2):
                lanes = pl.ds(pl.multiple_of(column + 128 * j, 128), 128)
                stage[slot, 0, :, lanes] = stage[slot, 0, :, lanes] + jnp.where(place == lane + 128 * j, wave, 0.0)

    def write(group, slot, part):
        rows = pl.ds(pl.multiple_of(8 * group, 8), 8)
        return pltpu.make_async_copy(stage.at[slot, part], out_ref.at[part, rows], sem.at[slot, part])

    for pair in range(2):
        p_pair, shift = shift_pair(0, pair)
        for part in range(2):
            make_windows(windows_a, p_pair, shift, pair, part)

    middle = HARM

    def two_groups(step, carry):
        for parity, (here, there) in enumerate(((windows_a, windows_b), (windows_b, windows_a))):
            group = 2 * step + parity
            slot = lax.rem(group, SLOTS)
            following = jnp.minimum(group + 1, GROUPS - 1)

            @pl.when(group >= SLOTS)
            def drain():
                for part in range(2):
                    write(group - SLOTS, slot, part).wait()

            for part in range(2):
                p_pair, shift = shift_pair(following, part)
                make_windows(there, p_pair, shift, part, 0)
                current = emit(here, slot, part, None, range(middle))
                make_windows(there, p_pair, shift, part, 1)
                emit(here, slot, part, current, range(middle, 2 * HARM))
                if part == 0:
                    add_waves(group, slot)
                write(group, slot, part).start()
        return carry

    lax.fori_loop(0, GROUPS // 2, two_groups, 0)
    for group in range(GROUPS - SLOTS, GROUPS):
        for part in range(2):
            write(group, group % SLOTS, part).wait()


def build(spec):
    return pl.pallas_call(
        build_kernel,
        out_shape=jax.ShapeDtypeStruct((2, ROWS_DEV, 2 * ORDERS), jnp.float32),
        in_specs=[pl.BlockSpec(memory_space=pltpu.VMEM)],
        out_specs=pl.BlockSpec(memory_space=pltpu.HBM),
        scratch_shapes=[
            pltpu.VMEM((2 * MAPS * TABLE, 512), jnp.bfloat16),
            pltpu.VMEM((2, 2, (LEAD + TABLE) * PITCH, 128), jnp.float32),
            pltpu.VMEM((2, 2, (LEAD + TABLE) * PITCH, 128), jnp.float32),
            pltpu.VMEM((SLOTS, 2, 8, 2 * ORDERS), jnp.float32),
            pltpu.SemaphoreType.DMA((SLOTS, 2)),
        ],
        compiler_params=pltpu.CompilerParams(vmem_limit_bytes=32 * 1024 * 1024),
        name="build",
    )(spec)


def shards(labels):
    spec = spectrum(labels, jnp.asarray(column_table()), jnp.asarray(row_table()))
    return build(spec)


def solution(mesh):
    return jax.shard_map(
        shards,
        mesh=mesh,
        in_specs=(P(("layer", "slab"), None),),
        out_specs=P(None, ("layer", "slab"), None),
        check_vma=False,
    )
```

```python
import jax
import jax.numpy as jnp
import numpy as np
from jax import lax
from jax.experimental import pallas as pl
from jax.experimental.pallas import tpu as pltpu
from jax.sharding import PartitionSpec as P

NMAP = 2048
HARM = 101
ORDERS = HARM * HARM
ROWS_DEV = 64
SLABS = 16
ROWS = NMAP // SLABS
SPACING = ORDERS // (ROWS_DEV * SLABS // 2)
HALF = 104
MAPROWS = 2 * HALF
OWN = 40
EDGE = 8
TOP = 8
EXT = ROWS + 2 * EDGE
PERMITS = (1.0, 2.1, 4.0, 12.1)
MAPS = 3
TABLE = 112
LEAD = 8
PITCH = 9
STRIPS = NMAP // 128
GROUPS = ROWS_DEV // 8
SLOTS = 4
CHIPS = SLABS // 2
PHASES = ((0, 0, 24), (SLABS * 24, 24, 16))


def split_numpy(table):
    high = table.astype(jnp.bfloat16)
    low = (table - high.astype(np.float64)).astype(jnp.bfloat16)
    return high, low


def column_table():
    freq = np.arange(HARM)[:, None]
    angle = 2.0 * np.pi * (freq * np.arange(NMAP)[None, :] % NMAP) / NMAP
    table = np.zeros((MAPROWS, NMAP))
    table[:HARM] = np.cos(angle)
    table[HALF : HALF + HARM] = -np.sin(angle)
    return np.concatenate(split_numpy(table))


def row_table():
    freq = np.arange(HARM)[None, :]
    angle = 2.0 * np.pi * (freq * np.arange(NMAP)[:, None] % NMAP) / NMAP
    table = np.zeros((NMAP, 256))
    table[:, :HARM] = np.cos(angle)
    table[:, 128 : 128 + HARM] = np.sin(angle)
    return np.stack(split_numpy(table / float(NMAP * NMAP)))


def split(value):
    high = value.astype(jnp.bfloat16)
    low = (value - high.astype(jnp.float32)).astype(jnp.bfloat16)
    return high, low


def dot_f32(a, b, contract):
    return lax.dot_general(a, b, (contract, ((), ())), preferred_element_type=jnp.float32)


def by_label(labels, values):
    low = jnp.where(labels == 0, jnp.float32(values[0]), jnp.float32(values[1]))
    high = jnp.where(labels == 2, jnp.float32(values[2]), jnp.float32(values[3]))
    return jnp.where(labels < 2, low, high)


def spectrum_kernel(
    labels_ref, col_hbm, row_hbm, out_ref, ext, smooth_a, smooth_b, fields, spec, gathered, col_ref, row_ref,
    load_sem, edge_send, edge_recv, spec_send, spec_recv, own_send, own_recv,
):
    me = lax.axis_index("slab")
    before = lax.rem(me + SLABS - 1, SLABS)
    after = lax.rem(me + 1, SLABS)

    load = pltpu.make_async_copy(labels_ref, ext.at[pl.ds(EDGE, ROWS)], load_sem.at[0])
    load.start()
    load_col = pltpu.make_async_copy(col_hbm, col_ref, load_sem.at[1])
    load_row = pltpu.make_async_copy(row_hbm, row_ref, load_sem.at[2])

    barrier = pltpu.get_barrier_semaphore()
    for step in range(1, SLABS):
        pl.semaphore_signal(barrier, inc=1, device_id={"slab": lax.rem(me + step, SLABS)})
    pl.semaphore_wait(barrier, SLABS - 1)

    up = pltpu.make_async_remote_copy(
        labels_ref.at[pl.ds(0, EDGE)], ext.at[pl.ds(EDGE + ROWS, EDGE)],
        edge_send.at[0], edge_recv.at[0], device_id={"slab": before},
    )
    down = pltpu.make_async_remote_copy(
        labels_ref.at[pl.ds(ROWS - EDGE, EDGE)], ext.at[pl.ds(0, EDGE)],
        edge_send.at[1], edge_recv.at[1], device_id={"slab": after},
    )
    up.start()
    down.start()
    load_col.start()
    load_row.start()

    def over_tiles(body, count, skip_at=None, skip=0, first=0):
        def step(i, carry):
            body(first + i if skip_at is None else first + i + jnp.where(i >= skip_at, skip, 0))
            return carry

        lax.fori_loop(0, count, step, 0)

    def to_permit(tile):
        r = pl.multiple_of(8 * tile, 8)
        for j in range(STRIPS):
            smooth_a[j, pl.ds(TOP + r, 8), :] = by_label(ext[pl.ds(r, 8), 128 * j : 128 * (j + 1)], PERMITS)

    def sides(mid, rows):
        lane = lax.broadcasted_iota(jnp.int32, (STRIPS, rows, 128), 2)
        flat = mid.reshape(STRIPS * rows, 128)
        ahead = pltpu.roll(flat, 127, 1).reshape(STRIPS, rows, 128)
        behind = pltpu.roll(flat, 1, 1).reshape(STRIPS, rows, 128)
        ahead = jnp.where(lane == 127, jnp.concatenate([ahead[1:], ahead[:1]], axis=0), ahead)
        behind = jnp.where(lane == 0, jnp.concatenate([behind[-1:], behind[:-1]], axis=0), behind)
        return behind, ahead

    def smooth_tile(src, dst):
        def body(tile):
            r = pl.multiple_of(TOP + 8 * tile, 8)
            mid = src[:, pl.ds(r, 8), :]
            behind, ahead = sides(mid, 8)
            around = src[:, pl.ds(r - 1, 8), :] + src[:, pl.ds(r + 1, 8), :] + behind + ahead
            dst[:, pl.ds(r, 8), :] = 0.5 * mid + 0.125 * around

        return body

    contrasts = [p - 1.0 / p for p in PERMITS]

    def make_fields(block):
        r = pl.multiple_of(16 * block, 16)
        at = pl.multiple_of(TOP + EDGE + r, 8)
        behind, ahead = sides(smooth_b[:, pl.ds(at, 16), :], 16)
        grad_x = 0.5 * (smooth_b[:, pl.ds(at + 1, 16), :] - smooth_b[:, pl.ds(at - 1, 16), :])
        grad_y = 0.5 * (ahead - behind)
        for j in range(STRIPS):
            lanes = slice(128 * j, 128 * (j + 1))
            labels = ext[pl.ds(pl.multiple_of(EDGE + r, 8), 16), lanes]
            permit = by_label(labels, PERMITS)
            gx, gy = grad_x[j], grad_y[j]
            factor = by_label(labels, contrasts) / (gx * gx + gy * gy + 1.0)
            along_x = factor * gx
            maps = (along_x * gy, permit - factor * gy * gy, along_x * gx - permit)
            for k in range(MAPS):
                high, low = split(maps[k])
                fields[k, 0, pl.ds(r, 16), lanes] = high
                fields[k, 1, pl.ds(r, 16), lanes] = low

    load.wait()
    over_tiles(to_permit, 16, first=1)
    over_tiles(smooth_tile(smooth_a, smooth_b), 14, first=2)
    over_tiles(smooth_tile(smooth_b, smooth_a), 12, first=3)
    over_tiles(smooth_tile(smooth_a, smooth_b), 10, first=4)
    over_tiles(make_fields, 4, first=2)
    up.wait()
    down.wait()
    over_tiles(to_permit, 2, 1, 16)
    over_tiles(smooth_tile(smooth_a, smooth_b), 4, 2, 14)
    over_tiles(smooth_tile(smooth_b, smooth_a), 6, 3, 12)
    over_tiles(smooth_tile(smooth_a, smooth_b), 8, 4, 10)
    over_tiles(make_fields, 4, 2, 4)

    def spec_copy(phase, step):
        to = lax.rem(me + step, SLABS)
        base, first, count = PHASES[phase]
        return pltpu.make_async_remote_copy(
            spec.at[pl.ds(pl.multiple_of(base + to * count, 8), count)],
            gathered.at[pl.ds(first, count), pl.ds(pl.multiple_of(me * ROWS, 128), ROWS)],
            spec_send.at[phase, step], spec_recv.at[phase, step], device_id={"slab": to},
        )

    def send_spec(phase):
        for step in sorted(range(1, SLABS), key=lambda step: abs(step - CHIPS)):
            spec_copy(phase, step).start()
        base, first, count = PHASES[phase]
        mine = spec[pl.ds(pl.multiple_of(base + me * count, 8), count), :]
        gathered[first : first + count, pl.ds(pl.multiple_of(me * ROWS, 128), ROWS)] = mine

    load_col.wait()
    spec[MAPROWS * MAPS :, :] = jnp.zeros((SLABS * OWN - MAPROWS * MAPS, ROWS), jnp.float32)
    for k in range(MAPS):
        product = dot_f32(col_ref[...], fields[k].reshape(2 * ROWS, NMAP), ((1,), (1,)))
        half = product[:, :ROWS] + product[:, ROWS:]
        spec[MAPROWS * k : MAPROWS * (k + 1), :] = half[:MAPROWS] + half[MAPROWS:]
        if k > 0:
            send_spec(k - 1)

    core = lax.rem(me, 2)
    chip = lax.div(me, 2)

    def own_copies(phase):
        base, _, count = PHASES[phase]

        def ship(slot, origin, to, sibling=False, first=0, size=count):
            start = base + (2 * lax.rem(chip + origin + CHIPS, CHIPS) + core) * count + first
            rows = out_ref.at[pl.ds(pl.multiple_of(start, 8), size)]
            target = me + 1 - 2 * core if sibling else 2 * lax.rem(chip + to + CHIPS, CHIPS) + core
            return pltpu.make_async_remote_copy(
                rows, rows, own_send.at[phase, slot], own_recv.at[phase, slot], device_id={"slab": target}
            )

        chips = [ship(i, 0, to) for i, to in enumerate((4, 3, -3, 2, -2, 1, -1))]
        siblings = [ship(7, 0, 0, True)] + [ship(8 + i, -to, 0, True) for i, to in enumerate((4, 3, -3, 2, -2, 1, -1))]
        return chips, siblings

    load_row.wait()
    contract = ((1,), (0,))
    chips, siblings = zip(*(own_copies(phase) for phase in range(2)))
    for phase, (base, first, count) in enumerate(PHASES):
        for step in range(1, SLABS):
            spec_copy(phase, step).wait_recv()
        high, low = split(gathered[first : first + count, :])
        out_ref[pl.ds(pl.multiple_of(base + me * count, 8), count), :] = (
            dot_f32(high, row_ref[0], contract) + dot_f32(low, row_ref[0], contract) + dot_f32(high, row_ref[1], contract)
        )
        for copy in chips[phase]:
            copy.start()
        siblings[phase][0].start()
    for phase in range(2):
        for i in (5, 6, 3, 4, 1, 2, 0):
            chips[phase][i].wait_recv()
            siblings[phase][1 + i].start()
    for phase in range(2):
        for step in range(1, SLABS):
            spec_copy(phase, step).wait_send()
        for copy in chips[phase]:
            copy.wait_send()
        for copy in siblings[phase]:
            copy.wait()


def spectrum(labels, col, row):
    vmem = pl.BlockSpec(memory_space=pltpu.VMEM)
    hbm = pl.BlockSpec(memory_space=pltpu.HBM)
    return pl.pallas_call(
        spectrum_kernel,
        out_shape=jax.ShapeDtypeStruct((SLABS * OWN, 256), jnp.float32),
        in_specs=[hbm, hbm, hbm],
        out_specs=vmem,
        scratch_shapes=[
            pltpu.VMEM((EXT, NMAP), jnp.int32),
            pltpu.VMEM((STRIPS, EXT + 2 * TOP, 128), jnp.float32),
            pltpu.VMEM((STRIPS, EXT + 2 * TOP, 128), jnp.float32),
            pltpu.VMEM((MAPS, 2, ROWS, NMAP), jnp.bfloat16),
            pltpu.VMEM((SLABS * OWN, ROWS), jnp.float32),
            pltpu.VMEM((OWN, NMAP), jnp.float32),
            pltpu.VMEM((2 * MAPROWS, NMAP), jnp.bfloat16),
            pltpu.VMEM((2, NMAP, 256), jnp.bfloat16),
            pltpu.SemaphoreType.DMA((3,)),
            pltpu.SemaphoreType.DMA((2,)),
            pltpu.SemaphoreType.DMA((2,)),
            pltpu.SemaphoreType.DMA((2, SLABS)),
            pltpu.SemaphoreType.DMA((2, SLABS)),
            pltpu.SemaphoreType.DMA((2, SLABS)),
            pltpu.SemaphoreType.DMA((2, SLABS)),
        ],
        compiler_params=pltpu.CompilerParams(
            collective_id=0, has_side_effects=True, vmem_limit_bytes=54016 * 1024
        ),
        name="spectrum",
    )(labels, col, row)


def sign_of(value):
    return jnp.where(value > 0, 1.0, jnp.where(value < 0, -1.0, 0.0))


def build_kernel(spec_ref, out_ref, toeplitz, windows_a, windows_b, stage, sem):
    first_order = lax.axis_index("slab") * (ROWS_DEV // 2)
    p_last = (first_order + ROWS_DEV // 2 - 1) * SPACING // HARM

    row = lax.broadcasted_iota(jnp.int32, (2 * TABLE, 256), 0)
    lane = lax.broadcasted_iota(jnp.int32, (2 * TABLE, 256), 1)
    m = p_last - jnp.where(row < TABLE, row, row - TABLE)
    from_cos = jnp.where(lane == jnp.abs(m), 1.0, 0.0)
    from_sin = jnp.where(lane == 128 + jnp.abs(m), sign_of(m), 0.0)
    pick = jnp.where(row < TABLE, from_cos, from_sin).astype(jnp.bfloat16)
    row = lax.broadcasted_iota(jnp.int32, (MAPROWS, 512), 0)
    lane = lax.broadcasted_iota(jnp.int32, (MAPROWS, 512), 1)
    n = HARM - 1 - (lane & 255)
    size = jnp.where(n >= 1 - HARM, jnp.abs(n), MAPROWS)
    even = jnp.where(row == size, 1.0, 0.0)
    uneven = jnp.where(row - HALF == size, sign_of(n), 0.0)
    mirror = jnp.where(lane < 256, even, uneven).astype(jnp.bfloat16)
    for k in range(MAPS):
        high, low = split(spec_ref[MAPROWS * k : MAPROWS * (k + 1), :])
        high, low = split(dot_f32(pick, high, ((1,), (1,))) + dot_f32(pick, low, ((1,), (1,))))
        product = dot_f32(high, mirror, ((1,), (0,))) + dot_f32(low, mirror, ((1,), (0,)))
        cos_rows, sin_rows = product[:TABLE], product[TABLE:]
        real = cos_rows[:, :256] + sin_rows[:, 256:]
        imag = cos_rows[:, 256:] - sin_rows[:, :256]
        for part, value in enumerate((real, imag)):
            rows = pl.ds((part * MAPS + k) * TABLE, TABLE)
            toeplitz[rows, :256], toeplitz[rows, 256:] = split(value)

    def shift_pair(group, pair):
        row = lax.broadcasted_iota(jnp.int32, (256, 256), 0)
        lane = lax.broadcasted_iota(jnp.int32, (256, 256), 1)
        orders = [(first_order + 4 * group + 2 * pair + j) * SPACING for j in range(2)]
        p_pair = [order // HARM for order in orders]
        q_pair = [order - p * HARM for order, p in zip(orders, p_pair)]
        source = jnp.where(lane < 128, lane - q_pair[0], lane - 128 - q_pair[1]) + HARM - 1
        shift = jnp.where(row == source, 1.0, 0.0).astype(jnp.bfloat16)
        shift = jnp.concatenate([shift, shift], axis=0)
        return p_pair, shift

    def make_windows(windows, p_pair, shift, pair, part):
        moved = dot_f32(toeplitz[part * MAPS * TABLE : (part + 1) * MAPS * TABLE, :], shift, ((1,), (0,)))
        for j in range(2):
            top = (LEAD - (p_last - p_pair[j])) * PITCH + 4 * pair + 2 * j
            cross_xy, right_up, left_low = (
                moved[k * TABLE : (k + 1) * TABLE, 128 * j : 128 * j + 128] for k in range(MAPS)
            )
            upper = pl.ds(top, TABLE, stride=PITCH)
            lower = pl.ds(top + 1, TABLE, stride=PITCH)
            windows[part, 0, upper, :] = cross_xy
            windows[part, 0, lower, :] = left_low
            windows[part, 1, upper, :] = right_up
            windows[part, 1, lower, :] = -cross_xy

    lane = lax.broadcasted_iota(jnp.int32, (8, 128), 1)
    sub = lax.broadcasted_iota(jnp.int32, (8, 128), 0)

    def emit(windows, slot, part, current, segments):
        for k in segments:
            half, p_j = divmod(k, HARM)
            tile, start = divmod(HARM * k, 128)
            segment = windows[part, half, (LEAD + p_j) * PITCH : (LEAD + p_j) * PITCH + 8, :]
            if start:
                segment = pltpu.roll(segment, start, 1)
                merged = jnp.where(lane < start, current, segment)
            else:
                merged = segment
            if start + HARM >= 128:
                stage[slot, part, :, 128 * tile : 128 * tile + 128] = merged
                current = segment
            else:
                current = merged
        if segments[-1] == 2 * HARM - 1:
            last = 2 * ORDERS // 128 * 128
            stage[slot, part, :, last:] = current[:, : 2 * ORDERS - last]
        return current

    def add_waves(group, slot):
        t0 = first_order + 4 * group
        order = (t0 + sub // 2) * SPACING
        p0 = t0 * SPACING // HARM
        p = jnp.where(order >= (p0 + 1) * HARM, p0 + 1, p0)
        q = order - p * HARM
        upper = sub % 2 == 0
        kx = 0.3 + 0.02 * (p - HARM // 2).astype(jnp.float32)
        ky = 0.2 + 0.02 * (q - HARM // 2).astype(jnp.float32)
        for half in range(2):
            if half == 0:
                wave = jnp.where(upper, kx * ky, ky * ky)
            else:
                wave = -jnp.where(upper, kx * kx, kx * ky)
            column = (t0 * SPACING + half * ORDERS) // 128 * 128
            place = order + half * ORDERS - column
            for j in range(2):
                lanes = pl.ds(pl.multiple_of(column + 128 * j, 128), 128)
                stage[slot, 0, :, lanes] = stage[slot, 0, :, lanes] + jnp.where(place == lane + 128 * j, wave, 0.0)

    def write(group, slot, part):
        rows = pl.ds(pl.multiple_of(8 * group, 8), 8)
        return pltpu.make_async_copy(stage.at[slot, part], out_ref.at[part, rows], sem.at[slot, part])

    for pair in range(2):
        p_pair, shift = shift_pair(0, pair)
        for part in range(2):
            make_windows(windows_a, p_pair, shift, pair, part)

    middle = HARM

    def two_groups(step, carry):
        for parity, (here, there) in enumerate(((windows_a, windows_b), (windows_b, windows_a))):
            group = 2 * step + parity
            slot = lax.rem(group, SLOTS)
            following = jnp.minimum(group + 1, GROUPS - 1)

            @pl.when(group >= SLOTS)
            def drain():
                for part in range(2):
                    write(group - SLOTS, slot, part).wait()

            for part in range(2):
                p_pair, shift = shift_pair(following, part)
                make_windows(there, p_pair, shift, part, 0)
                current = emit(here, slot, part, None, range(middle))
                make_windows(there, p_pair, shift, part, 1)
                emit(here, slot, part, current, range(middle, 2 * HARM))
                if part == 0:
                    add_waves(group, slot)
                write(group, slot, part).start()
        return carry

    lax.fori_loop(0, GROUPS // 2, two_groups, 0)
    for group in range(GROUPS - SLOTS, GROUPS):
        for part in range(2):
            write(group, group % SLOTS, part).wait()


def build(spec):
    return pl.pallas_call(
        build_kernel,
        out_shape=jax.ShapeDtypeStruct((2, ROWS_DEV, 2 * ORDERS), jnp.float32),
        in_specs=[pl.BlockSpec(memory_space=pltpu.VMEM)],
        out_specs=pl.BlockSpec(memory_space=pltpu.HBM),
        scratch_shapes=[
            pltpu.VMEM((2 * MAPS * TABLE, 512), jnp.bfloat16),
            pltpu.VMEM((2, 2, (LEAD + TABLE) * PITCH, 128), jnp.float32),
            pltpu.VMEM((2, 2, (LEAD + TABLE) * PITCH, 128), jnp.float32),
            pltpu.VMEM((SLOTS, 2, 8, 2 * ORDERS), jnp.float32),
            pltpu.SemaphoreType.DMA((SLOTS, 2)),
        ],
        compiler_params=pltpu.CompilerParams(vmem_limit_bytes=32 * 1024 * 1024),
        name="build",
    )(spec)


def shards(labels):
    spec = spectrum(labels, jnp.asarray(column_table()), jnp.asarray(row_table()))
    return build(spec)


def solution(mesh):
    return jax.shard_map(
        shards,
        mesh=mesh,
        in_specs=(P(("layer", "slab"), None),),
        out_specs=P(None, ("layer", "slab"), None),
        check_vma=False,
    )
```

```python
import jax
import jax.numpy as jnp
import numpy as np
from jax import lax
from jax.experimental import pallas as pl
from jax.experimental.pallas import tpu as pltpu
from jax.sharding import PartitionSpec as P

NMAP = 2048
HARM = 101
ORDERS = HARM * HARM
ROWS_DEV = 64
SLABS = 16
ROWS = NMAP // SLABS
SPACING = ORDERS // (ROWS_DEV * SLABS // 2)
HALF = 104
MAPROWS = 2 * HALF
OWN = 40
EDGE = 8
TOP = 8
EXT = ROWS + 2 * EDGE
PERMITS = (1.0, 2.1, 4.0, 12.1)
MAPS = 3
TABLE = 112
LEAD = 8
PITCH = 9
STRIPS = NMAP // 128
GROUPS = ROWS_DEV // 8
SLOTS = 4
CHIPS = SLABS // 2
PHASES = ((0, 0, 24), (SLABS * 24, 24, 16))


def split_numpy(table):
    high = table.astype(jnp.bfloat16)
    low = (table - high.astype(np.float64)).astype(jnp.bfloat16)
    return high, low


def column_table():
    freq = np.arange(HARM)[:, None]
    angle = 2.0 * np.pi * (freq * np.arange(NMAP)[None, :] % NMAP) / NMAP
    table = np.zeros((MAPROWS, NMAP))
    table[:HARM] = np.cos(angle)
    table[HALF : HALF + HARM] = -np.sin(angle)
    return np.concatenate(split_numpy(table))


def row_table():
    freq = np.arange(HARM)[None, :]
    angle = 2.0 * np.pi * (freq * np.arange(NMAP)[:, None] % NMAP) / NMAP
    table = np.zeros((NMAP, 256))
    table[:, :HARM] = np.cos(angle)
    table[:, 128 : 128 + HARM] = np.sin(angle)
    return np.stack(split_numpy(table / float(NMAP * NMAP)))


def split(value):
    high = value.astype(jnp.bfloat16)
    low = (value - high.astype(jnp.float32)).astype(jnp.bfloat16)
    return high, low


def dot_f32(a, b, contract):
    return lax.dot_general(a, b, (contract, ((), ())), preferred_element_type=jnp.float32)


def by_label(labels, values):
    low = jnp.where(labels == 0, jnp.float32(values[0]), jnp.float32(values[1]))
    high = jnp.where(labels == 2, jnp.float32(values[2]), jnp.float32(values[3]))
    return jnp.where(labels < 2, low, high)


def spectrum_kernel(
    labels_ref, col_hbm, row_hbm, out_ref, ext, smooth_a, smooth_b, fields, spec, gathered, col_ref, row_ref,
    load_sem, edge_send, edge_recv, spec_send, spec_recv, own_send, own_recv,
):
    me = lax.axis_index("slab")
    before = lax.rem(me + SLABS - 1, SLABS)
    after = lax.rem(me + 1, SLABS)

    load = pltpu.make_async_copy(labels_ref, ext.at[pl.ds(EDGE, ROWS)], load_sem.at[0])
    load.start()
    load_col = pltpu.make_async_copy(col_hbm, col_ref, load_sem.at[1])
    load_row = pltpu.make_async_copy(row_hbm, row_ref, load_sem.at[2])

    barrier = pltpu.get_barrier_semaphore()
    for step in range(1, SLABS):
        pl.semaphore_signal(barrier, inc=1, device_id={"slab": lax.rem(me + step, SLABS)})
    pl.semaphore_wait(barrier, SLABS - 1)

    up = pltpu.make_async_remote_copy(
        labels_ref.at[pl.ds(0, EDGE)], ext.at[pl.ds(EDGE + ROWS, EDGE)],
        edge_send.at[0], edge_recv.at[0], device_id={"slab": before},
    )
    down = pltpu.make_async_remote_copy(
        labels_ref.at[pl.ds(ROWS - EDGE, EDGE)], ext.at[pl.ds(0, EDGE)],
        edge_send.at[1], edge_recv.at[1], device_id={"slab": after},
    )
    up.start()
    down.start()
    load_col.start()
    load_row.start()

    def over_tiles(body, count, skip_at=None, skip=0, first=0):
        def step(i, carry):
            body(first + i if skip_at is None else first + i + jnp.where(i >= skip_at, skip, 0))
            return carry

        lax.fori_loop(0, count, step, 0, unroll=2 if body is make_fields else count // 2)

    def to_permit(tile):
        r = pl.multiple_of(8 * tile, 8)
        for j in range(STRIPS):
            smooth_a[j, pl.ds(TOP + r, 8), :] = by_label(ext[pl.ds(r, 8), 128 * j : 128 * (j + 1)], PERMITS)

    def sides(mid, rows):
        lane = lax.broadcasted_iota(jnp.int32, (STRIPS, rows, 128), 2)
        flat = mid.reshape(STRIPS * rows, 128)
        ahead = pltpu.roll(flat, 127, 1).reshape(STRIPS, rows, 128)
        behind = pltpu.roll(flat, 1, 1).reshape(STRIPS, rows, 128)
        ahead = jnp.where(lane == 127, jnp.concatenate([ahead[1:], ahead[:1]], axis=0), ahead)
        behind = jnp.where(lane == 0, jnp.concatenate([behind[-1:], behind[:-1]], axis=0), behind)
        return behind, ahead

    def smooth_tile(src, dst):
        def body(tile):
            r = pl.multiple_of(TOP + 8 * tile, 8)
            mid = src[:, pl.ds(r, 8), :]
            behind, ahead = sides(mid, 8)
            around = src[:, pl.ds(r - 1, 8), :] + src[:, pl.ds(r + 1, 8), :] + behind + ahead
            dst[:, pl.ds(r, 8), :] = 0.5 * mid + 0.125 * around

        return body

    contrasts = [p - 1.0 / p for p in PERMITS]

    def make_fields(block):
        r = pl.multiple_of(16 * block, 16)
        at = pl.multiple_of(TOP + EDGE + r, 8)
        behind, ahead = sides(smooth_b[:, pl.ds(at, 16), :], 16)
        grad_x = 0.5 * (smooth_b[:, pl.ds(at + 1, 16), :] - smooth_b[:, pl.ds(at - 1, 16), :])
        grad_y = 0.5 * (ahead - behind)
        for j in range(STRIPS):
            lanes = slice(128 * j, 128 * (j + 1))
            labels = ext[pl.ds(pl.multiple_of(EDGE + r, 8), 16), lanes]
            permit = by_label(labels, PERMITS)
            gx, gy = grad_x[j], grad_y[j]
            factor = by_label(labels, contrasts) / (gx * gx + gy * gy + 1.0)
            along_x = factor * gx
            maps = (along_x * gy, permit - factor * gy * gy, along_x * gx - permit)
            for k in range(MAPS):
                high, low = split(maps[k])
                fields[k, 0, pl.ds(r, 16), lanes] = high
                fields[k, 1, pl.ds(r, 16), lanes] = low

    load.wait()
    over_tiles(to_permit, 16, first=1)
    over_tiles(smooth_tile(smooth_a, smooth_b), 14, first=2)
    over_tiles(smooth_tile(smooth_b, smooth_a), 12, first=3)
    over_tiles(smooth_tile(smooth_a, smooth_b), 10, first=4)
    over_tiles(make_fields, 4, first=2)
    up.wait()
    down.wait()
    over_tiles(to_permit, 2, 1, 16)
    over_tiles(smooth_tile(smooth_a, smooth_b), 4, 2, 14)
    over_tiles(smooth_tile(smooth_b, smooth_a), 6, 3, 12)
    over_tiles(smooth_tile(smooth_a, smooth_b), 8, 4, 10)
    over_tiles(make_fields, 4, 2, 4)

    def spec_copy(phase, step):
        to = lax.rem(me + step, SLABS)
        base, first, count = PHASES[phase]
        return pltpu.make_async_remote_copy(
            spec.at[pl.ds(pl.multiple_of(base + to * count, 8), count)],
            gathered.at[pl.ds(first, count), pl.ds(pl.multiple_of(me * ROWS, 128), ROWS)],
            spec_send.at[phase, step], spec_recv.at[phase, step], device_id={"slab": to},
        )

    def send_spec(phase):
        for step in sorted(range(1, SLABS), key=lambda step: abs(step - CHIPS)):
            spec_copy(phase, step).start()
        base, first, count = PHASES[phase]
        mine = spec[pl.ds(pl.multiple_of(base + me * count, 8), count), :]
        gathered[first : first + count, pl.ds(pl.multiple_of(me * ROWS, 128), ROWS)] = mine

    load_col.wait()
    spec[MAPROWS * MAPS :, :] = jnp.zeros((SLABS * OWN - MAPROWS * MAPS, ROWS), jnp.float32)
    for k in range(MAPS):
        product = dot_f32(col_ref[...], fields[k].reshape(2 * ROWS, NMAP), ((1,), (1,)))
        half = product[:, :ROWS] + product[:, ROWS:]
        spec[MAPROWS * k : MAPROWS * (k + 1), :] = half[:MAPROWS] + half[MAPROWS:]
        if k > 0:
            send_spec(k - 1)

    core = lax.rem(me, 2)
    chip = lax.div(me, 2)

    def own_copies(phase):
        base, _, count = PHASES[phase]

        def ship(slot, origin, to, sibling=False, first=0, size=count):
            start = base + (2 * lax.rem(chip + origin + CHIPS, CHIPS) + core) * count + first
            rows = out_ref.at[pl.ds(pl.multiple_of(start, 8), size)]
            target = me + 1 - 2 * core if sibling else 2 * lax.rem(chip + to + CHIPS, CHIPS) + core
            return pltpu.make_async_remote_copy(
                rows, rows, own_send.at[phase, slot], own_recv.at[phase, slot], device_id={"slab": target}
            )

        chips = [ship(i, 0, to) for i, to in enumerate((4, 3, -3, 2, -2, 1, -1))]
        siblings = [ship(7, 0, 0, True)] + [ship(8 + i, -to, 0, True) for i, to in enumerate((4, 3, -3, 2, -2, 1, -1))]
        return chips, siblings

    load_row.wait()
    contract = ((1,), (0,))
    chips, siblings = zip(*(own_copies(phase) for phase in range(2)))
    for phase, (base, first, count) in enumerate(PHASES):
        for step in range(1, SLABS):
            spec_copy(phase, step).wait_recv()
        high, low = split(gathered[first : first + count, :])
        out_ref[pl.ds(pl.multiple_of(base + me * count, 8), count), :] = (
            dot_f32(high, row_ref[0], contract) + dot_f32(low, row_ref[0], contract) + dot_f32(high, row_ref[1], contract)
        )
        for copy in chips[phase]:
            copy.start()
        siblings[phase][0].start()
    for phase in range(2):
        for i in (5, 6, 3, 4, 1, 2, 0):
            chips[phase][i].wait_recv()
            siblings[phase][1 + i].start()
    for phase in range(2):
        for step in range(1, SLABS):
            spec_copy(phase, step).wait_send()
        for copy in chips[phase]:
            copy.wait_send()
        for copy in siblings[phase]:
            copy.wait()


def spectrum(labels, col, row):
    vmem = pl.BlockSpec(memory_space=pltpu.VMEM)
    hbm = pl.BlockSpec(memory_space=pltpu.HBM)
    return pl.pallas_call(
        spectrum_kernel,
        out_shape=jax.ShapeDtypeStruct((SLABS * OWN, 256), jnp.float32),
        in_specs=[hbm, hbm, hbm],
        out_specs=vmem,
        scratch_shapes=[
            pltpu.VMEM((EXT, NMAP), jnp.int32),
            pltpu.VMEM((STRIPS, EXT + 2 * TOP, 128), jnp.float32),
            pltpu.VMEM((STRIPS, EXT + 2 * TOP, 128), jnp.float32),
            pltpu.VMEM((MAPS, 2, ROWS, NMAP), jnp.bfloat16),
            pltpu.VMEM((SLABS * OWN, ROWS), jnp.float32),
            pltpu.VMEM((OWN, NMAP), jnp.float32),
            pltpu.VMEM((2 * MAPROWS, NMAP), jnp.bfloat16),
            pltpu.VMEM((2, NMAP, 256), jnp.bfloat16),
            pltpu.SemaphoreType.DMA((3,)),
            pltpu.SemaphoreType.DMA((2,)),
            pltpu.SemaphoreType.DMA((2,)),
            pltpu.SemaphoreType.DMA((2, SLABS)),
            pltpu.SemaphoreType.DMA((2, SLABS)),
            pltpu.SemaphoreType.DMA((2, SLABS)),
            pltpu.SemaphoreType.DMA((2, SLABS)),
        ],
        compiler_params=pltpu.CompilerParams(
            collective_id=0, has_side_effects=True, vmem_limit_bytes=54016 * 1024
        ),
        name="spectrum",
    )(labels, col, row)


def sign_of(value):
    return jnp.where(value > 0, 1.0, jnp.where(value < 0, -1.0, 0.0))


def build_kernel(spec_ref, out_ref, toeplitz, windows_a, windows_b, stage, sem):
    first_order = lax.axis_index("slab") * (ROWS_DEV // 2)
    p_last = (first_order + ROWS_DEV // 2 - 1) * SPACING // HARM

    row = lax.broadcasted_iota(jnp.int32, (2 * TABLE, 256), 0)
    lane = lax.broadcasted_iota(jnp.int32, (2 * TABLE, 256), 1)
    m = p_last - jnp.where(row < TABLE, row, row - TABLE)
    from_cos = jnp.where(lane == jnp.abs(m), 1.0, 0.0)
    from_sin = jnp.where(lane == 128 + jnp.abs(m), sign_of(m), 0.0)
    pick = jnp.where(row < TABLE, from_cos, from_sin).astype(jnp.bfloat16)
    row = lax.broadcasted_iota(jnp.int32, (MAPROWS, 512), 0)
    lane = lax.broadcasted_iota(jnp.int32, (MAPROWS, 512), 1)
    n = HARM - 1 - (lane & 255)
    size = jnp.where(n >= 1 - HARM, jnp.abs(n), MAPROWS)
    even = jnp.where(row == size, 1.0, 0.0)
    uneven = jnp.where(row - HALF == size, sign_of(n), 0.0)
    mirror = jnp.where(lane < 256, even, uneven).astype(jnp.bfloat16)
    for k in range(MAPS):
        high, low = split(spec_ref[MAPROWS * k : MAPROWS * (k + 1), :])
        high, low = split(dot_f32(pick, high, ((1,), (1,))) + dot_f32(pick, low, ((1,), (1,))))
        product = dot_f32(high, mirror, ((1,), (0,))) + dot_f32(low, mirror, ((1,), (0,)))
        cos_rows, sin_rows = product[:TABLE], product[TABLE:]
        real = cos_rows[:, :256] + sin_rows[:, 256:]
        imag = cos_rows[:, 256:] - sin_rows[:, :256]
        for part, value in enumerate((real, imag)):
            rows = pl.ds((part * MAPS + k) * TABLE, TABLE)
            toeplitz[rows, :256], toeplitz[rows, 256:] = split(value)

    def shift_pair(group, pair):
        row = lax.broadcasted_iota(jnp.int32, (256, 256), 0)
        lane = lax.broadcasted_iota(jnp.int32, (256, 256), 1)
        orders = [(first_order + 4 * group + 2 * pair + j) * SPACING for j in range(2)]
        p_pair = [order // HARM for order in orders]
        q_pair = [order - p * HARM for order, p in zip(orders, p_pair)]
        source = jnp.where(lane < 128, lane - q_pair[0], lane - 128 - q_pair[1]) + HARM - 1
        shift = jnp.where(row == source, 1.0, 0.0).astype(jnp.bfloat16)
        shift = jnp.concatenate([shift, shift], axis=0)
        return p_pair, shift

    def make_windows(windows, p_pair, shift, pair, part):
        moved = dot_f32(toeplitz[part * MAPS * TABLE : (part + 1) * MAPS * TABLE, :], shift, ((1,), (0,)))
        for j in range(2):
            top = (LEAD - (p_last - p_pair[j])) * PITCH + 4 * pair + 2 * j
            cross_xy, right_up, left_low = (
                moved[k * TABLE : (k + 1) * TABLE, 128 * j : 128 * j + 128] for k in range(MAPS)
            )
            upper = pl.ds(top, TABLE, stride=PITCH)
            lower = pl.ds(top + 1, TABLE, stride=PITCH)
            windows[part, 0, upper, :] = cross_xy
            windows[part, 0, lower, :] = left_low
            windows[part, 1, upper, :] = right_up
            windows[part, 1, lower, :] = -cross_xy

    lane = lax.broadcasted_iota(jnp.int32, (8, 128), 1)
    sub = lax.broadcasted_iota(jnp.int32, (8, 128), 0)

    def emit(windows, slot, part, current, segments):
        for k in segments:
            half, p_j = divmod(k, HARM)
            tile, start = divmod(HARM * k, 128)
            segment = windows[part, half, (LEAD + p_j) * PITCH : (LEAD + p_j) * PITCH + 8, :]
            if start:
                segment = pltpu.roll(segment, start, 1)
                merged = jnp.where(lane < start, current, segment)
            else:
                merged = segment
            if start + HARM >= 128:
                stage[slot, part, :, 128 * tile : 128 * tile + 128] = merged
                current = segment
            else:
                current = merged
        if segments[-1] == 2 * HARM - 1:
            last = 2 * ORDERS // 128 * 128
            stage[slot, part, :, last:] = current[:, : 2 * ORDERS - last]
        return current

    def add_waves(group, slot):
        t0 = first_order + 4 * group
        order = (t0 + sub // 2) * SPACING
        p0 = t0 * SPACING // HARM
        p = jnp.where(order >= (p0 + 1) * HARM, p0 + 1, p0)
        q = order - p * HARM
        upper = sub % 2 == 0
        kx = 0.3 + 0.02 * (p - HARM // 2).astype(jnp.float32)
        ky = 0.2 + 0.02 * (q - HARM // 2).astype(jnp.float32)
        for half in range(2):
            if half == 0:
                wave = jnp.where(upper, kx * ky, ky * ky)
            else:
                wave = -jnp.where(upper, kx * kx, kx * ky)
            column = (t0 * SPACING + half * ORDERS) // 128 * 128
            place = order + half * ORDERS - column
            for j in range(2):
                lanes = pl.ds(pl.multiple_of(column + 128 * j, 128), 128)
                stage[slot, 0, :, lanes] = stage[slot, 0, :, lanes] + jnp.where(place == lane + 128 * j, wave, 0.0)

    def write(group, slot, part):
        rows = pl.ds(pl.multiple_of(8 * group, 8), 8)
        return pltpu.make_async_copy(stage.at[slot, part], out_ref.at[part, rows], sem.at[slot, part])

    for pair in range(2):
        p_pair, shift = shift_pair(0, pair)
        for part in range(2):
            make_windows(windows_a, p_pair, shift, pair, part)

    middle = HARM

    def two_groups(step, carry):
        for parity, (here, there) in enumerate(((windows_a, windows_b), (windows_b, windows_a))):
            group = 2 * step + parity
            slot = lax.rem(group, SLOTS)
            following = jnp.minimum(group + 1, GROUPS - 1)

            @pl.when(group >= SLOTS)
            def drain():
                for part in range(2):
                    write(group - SLOTS, slot, part).wait()

            for part in range(2):
                p_pair, shift = shift_pair(following, part)
                make_windows(there, p_pair, shift, part, 0)
                current = emit(here, slot, part, None, range(middle))
                make_windows(there, p_pair, shift, part, 1)
                emit(here, slot, part, current, range(middle, 2 * HARM))
                if part == 0:
                    add_waves(group, slot)
                write(group, slot, part).start()
        return carry

    lax.fori_loop(0, GROUPS // 2, two_groups, 0)
    for group in range(GROUPS - SLOTS, GROUPS):
        for part in range(2):
            write(group, group % SLOTS, part).wait()


def build(spec):
    return pl.pallas_call(
        build_kernel,
        out_shape=jax.ShapeDtypeStruct((2, ROWS_DEV, 2 * ORDERS), jnp.float32),
        in_specs=[pl.BlockSpec(memory_space=pltpu.VMEM)],
        out_specs=pl.BlockSpec(memory_space=pltpu.HBM),
        scratch_shapes=[
            pltpu.VMEM((2 * MAPS * TABLE, 512), jnp.bfloat16),
            pltpu.VMEM((2, 2, (LEAD + TABLE) * PITCH, 128), jnp.float32),
            pltpu.VMEM((2, 2, (LEAD + TABLE) * PITCH, 128), jnp.float32),
            pltpu.VMEM((SLOTS, 2, 8, 2 * ORDERS), jnp.float32),
            pltpu.SemaphoreType.DMA((SLOTS, 2)),
        ],
        compiler_params=pltpu.CompilerParams(vmem_limit_bytes=32 * 1024 * 1024),
        name="build",
    )(spec)


def shards(labels):
    spec = spectrum(labels, jnp.asarray(column_table()), jnp.asarray(row_table()))
    return build(spec)


def solution(mesh):
    return jax.shard_map(
        shards,
        mesh=mesh,
        in_specs=(P(("layer", "slab"), None),),
        out_specs=P(None, ("layer", "slab"), None),
        check_vma=False,
    )
```
